256 devices in a mesh: ctx: 16 (over z, core), tp: 4 (over y), dec: 4 (over x).
Axes of the slice: x: 4, y: 4, z: 8, core: 2. Of those that a mesh axis runs over, the one named last changes fastest.
Arguments:
- x_input: bfloat16 [4, 4096, 16384], P('dec', 'ctx', 'tp'), may hold values from -3 to 3
- b_input: bfloat16 [4, 4096, 2048], P('dec', 'ctx', 'tp'), may hold values from -6 to 6
- output_projection_input: bfloat16 [4, 4096, 2048], P('dec', 'ctx', 'tp'), may hold values from -6 to 6
- step_input: bfloat16 [4, 4096, 256], P('dec', 'ctx', 'tp'), may hold values from -3 to 13
- gate_input: bfloat16 [4, 4096, 16384], P('dec', 'ctx', 'tp'), may hold values from -6 to 6
- kernel_x: bfloat16 [4, 16384], P(None, 'tp'), may hold values from -3 to 3
- kernel_b: bfloat16 [4, 2048], P(None, 'tp'), may hold values from -3 to 3
- kernel_c: bfloat16 [4, 2048], P(None, 'tp'), may hold values from -3 to 3
- step_bias: float32 [256], P('tp'), may hold values from -2 to 1
- fading_logarithm: float32 [256], P('tp'), may hold values from -13 to -2
- norm_gain: float32 [16384], P('tp'), may hold values from 0.25 to 1.75
- owner_map: int32 [4, 256, 1], P('dec', 'tp'), may hold values from 0 to 3; in each aligned block of 4 rows (0 to 3, 4 to 7, ..., all dimensions but the last counted through in order) at most 2 rows name the same one
Outputs:
- mixer_output: bfloat16 [4, 4096, 16384], P('dec', 'ctx', 'tp')
- decode_state: float32 [4, 4, 64, 2, 64, 256], P('dec', None, ('tp', 'ctx'))
The draws below stay inside these ranges and needn't reach their ends.
Inputs may be any that keep to these rules, and one draw needn't show every extreme that they name: `owner_map`: in every block of 4 heads of one prompt starting at a multiple of 4, at most 2 heads name the same decode device.
All inputs are finite; a program needn't handle non-finite values.
Results may differ from the reference program's by a relative error of at most 0.009.
Values may be sent and summed in bfloat16 or wider, within the bound.
No kernel may reach another device: no remote copies, remote signals or barrier semaphores. Data moves between devices by JAX's collectives and lax.ppermute only.
A program may use at most 192 MiB of HBM per device.

```python
import math
import jax
import jax.numpy as jnp
import numpy as np
from jax import lax

HEADS = 256
HEAD_DIM = 64
STATE = 256
GROUPS = 8
KCONV = 4
STRETCH = 256
QUERY_SPAN = 4096
PROMPTS = 4
HB = 4
CAP = 2
N_DEC = 4


def draw_step_input(key, part):
    key = jax.random.fold_in(key, 11)
    first, second = jax.random.split(key)
    starting_index_shift = jnp.clip(0.6 * jax.random.normal(first, (PROMPTS, QUERY_SPAN, HEADS), jnp.float32), -3.0, 3.0)
    destination_places = jax.random.randint(second, (PROMPTS, 1, 4), 0, QUERY_SPAN)
    transfer_bundles = jnp.sum((jnp.arange(QUERY_SPAN)[None, :, None] == destination_places).astype(jnp.float32), axis=2, keepdims=True)
    return (starting_index_shift + 2.5 * transfer_bundles).astype(jnp.bfloat16)


def draw_fading_logarithm(key, part):
    key = jax.random.fold_in(key, 23)
    first, second, third = jax.random.split(key, 3)
    slow_share = 0.5
    slow_heads = jax.random.uniform(first, (HEADS,), jnp.float32) < slow_share
    slow_rate = jax.random.uniform(second, (HEADS,), jnp.float32, 0.3, 1.0) / QUERY_SPAN
    fast_rate = jnp.exp(jax.random.uniform(third, (HEADS,), jnp.float32, math.log(0.02), math.log(0.06)))
    return jnp.log(jnp.where(slow_heads, slow_rate, fast_rate))


def block_scale(stream_key, extent, cuts, low, top_value):
    factor_of, own = 1.0, jax.random.fold_in(stream_key, 6)
    for position, shards_of in cuts:
        draws = jnp.exp(jax.random.uniform(jax.random.fold_in(own, position), (shards_of,), jnp.float32, low / len(cuts), top_value / len(cuts)))
        factor_of = factor_of * jnp.repeat(draws, extent[position] // shards_of).reshape([-1 if axis == position else 1 for axis in range(len(extent))])
    return factor_of


def deal_out(own_key, own, number, rows, amount, top, most, slope):
    sequence = jax.random.permutation(own_key, amount)
    crowded, ordinary = load_shares(amount, rows * top, most, slope, True), load_shares(amount, rows * top, most, slope, False)
    places = jnp.arange(amount)

    def named(sizes, rotation):
        used = int((sizes > 0).sum())
        fixed = max(1, used // 4)
        moved = fixed + (places - fixed + rotation * (used - fixed)) % max(1, amount - fixed)
        return jnp.zeros((amount,), jnp.int32).at[sequence[jnp.where(places < fixed, places, moved)]].set(jnp.asarray(sizes, jnp.int32))

    sizes = jnp.where(number % 4 == 0, named(crowded, number // 4), named(ordinary, number - number // 4 - 1))
    mixed = jax.random.permutation(jax.random.fold_in(own, 3), amount)
    donor, sink = mixed[0:amount // 2 * 2:2], mixed[1:amount // 2 * 2:2]
    room = jnp.minimum(sizes[donor] - 1, most - sizes[sink]) // 2
    room = jnp.where((donor == sequence[0]) | (sink == sequence[0]) | (sizes[sink] == 0), 0, jnp.maximum(room, 0))
    moved = jax.random.randint(jax.random.fold_in(own, 4), (amount // 2,), 0, 1 << 20) % (room + 1)
    sizes = sizes.at[donor].add(-moved).at[sink].add(moved)
    items = jnp.searchsorted(jnp.cumsum(sizes), jnp.arange(rows * top), side="right").astype(jnp.int32)
    table = items.reshape(top, rows).T
    table = table[jax.random.permutation(jax.random.fold_in(own, 1), rows)]
    rotation = jax.random.randint(jax.random.fold_in(own, 2), (rows, 1), 0, top)
    return jnp.take_along_axis(table, (jnp.arange(top)[None, :] + rotation) % top, axis=1)


def load_shares(number_of, total, limit, lean, full):
    loads = [(1 << 20) // math.isqrt(standing ** lean) + 1 for standing in range(1, number_of + 1)]
    largest = limit if full else min(limit, max(-(-total // number_of), total * loads[0] // sum(loads)))
    least = 1 if total - largest >= number_of - 1 else 0
    counts, rest = [largest] + [least] * (number_of - 1), total - largest - least * (number_of - 1)
    while rest > 0:
        candidates = [i for i in range(1, number_of) if counts[i] < largest] or [i for i in range(1, number_of) if counts[i] < limit]
        whole, remaining = sum([loads[i] for i in candidates]), rest
        for i in candidates:
            more = min(limit - counts[i], max(1, remaining * loads[i] // whole), rest)
            counts[i] = counts[i] + more
            rest = rest - more
    return np.array(counts)


def gaussian(own_key, shape, spread, most, cuts=(), dtype=jnp.bfloat16):
    level = block_scale(own_key, shape, cuts, -0.22, 0.18) if cuts else 1.0
    drawn = jax.random.normal(own_key, shape, jnp.float32) * spread * level
    return jnp.minimum(jnp.maximum(drawn, -most), most).astype(dtype)


def setup_inputs(seed: int = 0) -> dict:
    keys = jax.random.split(jax.random.key(seed), 13)
    x_input = gaussian(keys[0], (PROMPTS, QUERY_SPAN, HEADS * HEAD_DIM), 0.5, 3.0, ((0, 4), (1, 16), (2, 4)))
    b_input = gaussian(keys[1], (PROMPTS, QUERY_SPAN, GROUPS * STATE), 1.0, 6.0, ((0, 4), (1, 16), (2, 4)))
    output_projection_input = gaussian(keys[2], (PROMPTS, QUERY_SPAN, GROUPS * STATE), 1.0, 6.0, ((0, 4), (1, 16), (2, 4)))
    step_input = draw_step_input(jax.random.fold_in(keys[12], 71), 0)
    gate_input = gaussian(keys[4], (PROMPTS, QUERY_SPAN, HEADS * HEAD_DIM), 1.0, 6.0, ((0, 4), (1, 16), (2, 4)))
    kernel_x = gaussian(keys[5], (KCONV, HEADS * HEAD_DIM), KCONV ** -0.5, 3.0, ((1, 4),))
    kernel_b = gaussian(keys[6], (KCONV, GROUPS * STATE), KCONV ** -0.5, 3.0, ((1, 4),))
    kernel_c = gaussian(keys[7], (KCONV, GROUPS * STATE), KCONV ** -0.5, 3.0, ((1, 4),))
    step_bias = jnp.clip(-2.0 + 3.0 * jax.random.uniform(keys[8], (HEADS,), jnp.float32) ** block_scale(keys[8], (HEADS,), ((0, 4),), -0.2, 0.2), -2.0, 1.0)
    fading_logarithm = draw_fading_logarithm(jax.random.fold_in(keys[12], 71), 0)
    norm_gain = jnp.clip(1.0 + 0.15 * jax.random.normal(keys[10], (HEADS * HEAD_DIM,), jnp.float32), 0.25, 1.75)
    owner_map_keys = jax.random.split(jax.random.fold_in(keys[11], 1), PROMPTS * HEADS // HB)
    owner_map_turns = jax.random.permutation(jax.random.fold_in(keys[11], 3), PROMPTS * HEADS // HB)
    owner_map = jax.vmap(lambda own, number: deal_out(jax.random.fold_in(keys[11], 2), own, number, HB, N_DEC, 1, CAP, 0))(owner_map_keys, owner_map_turns).reshape((PROMPTS, HEADS, 1))
    return dict(x_input=x_input, b_input=b_input, output_projection_input=output_projection_input, step_input=step_input, gate_input=gate_input, kernel_x=kernel_x, kernel_b=kernel_b, kernel_c=kernel_c, step_bias=step_bias, fading_logarithm=fading_logarithm, norm_gain=norm_gain, owner_map=owner_map)


epsilon = 1e-05

def causal_filter(sequence_lines, prior_rows, kernel):
    taps_count = kernel.shape[0]
    length_now = sequence_lines.shape[0]
    padded = jnp.concatenate([prior_rows, sequence_lines], axis=0).astype(jnp.float32)
    running = jnp.zeros(sequence_lines.shape, jnp.float32)
    for offset in range(taps_count):
        running = running + kernel[offset].astype(jnp.float32) * padded[offset:offset + length_now]
    return jax.nn.silu(running).astype(jnp.bfloat16)

def state_blocks(x_conv, b_conv, c_conv, step_size, decay_rate, initial, block_len):
    head_count, head_width, state_width = initial.shape
    count_of_groups = b_conv.shape[1] // state_width
    per_group = head_count // count_of_groups
    block_count = x_conv.shape[0] // block_len
    x_blocks = x_conv.reshape(block_count, block_len, count_of_groups, per_group, head_width)
    b_blocks = b_conv.reshape(block_count, block_len, count_of_groups, state_width)
    c_blocks = c_conv.reshape(block_count, block_len, count_of_groups, state_width)
    s_blocks = step_size.reshape(block_count, block_len, count_of_groups, per_group)
    rate_grid = decay_rate.reshape(count_of_groups, per_group)
    causal = jnp.arange(block_len)[:, None] >= jnp.arange(block_len)[None, :]
    highest = lax.Precision.HIGHEST

    def advance(carried, pieces):
        signal_tile, b_block, c_block, s_block = pieces
        cumulative = jnp.cumsum(s_block * rate_grid, axis=0)
        closing = cumulative[-1]
        scores = jnp.einsum('qgn,sgn->gqs', c_block.astype(jnp.float32), b_block.astype(jnp.float32), precision=highest)
        gaps = cumulative[:, None] - cumulative[None, :]
        decays = jnp.exp(jnp.where(causal[:, :, None, None], gaps, -jnp.inf))
        decays = jnp.transpose(decays, (2, 3, 0, 1))
        steps_t = jnp.transpose(s_block, (1, 2, 0))[:, :, None, :]
        block_weights = (scores[:, None] * decays * steps_t).astype(jnp.bfloat16)
        intra = jnp.einsum('ghqs,sghp->qghp', block_weights.astype(jnp.float32), signal_tile.astype(jnp.float32), precision=highest)
        inter = jnp.einsum('qgn,ghpn->qghp', c_block.astype(jnp.float32), carried, precision=highest) * jnp.exp(cumulative)[:, :, :, None]
        outputs = intra + inter
        block_inputs = (signal_tile.astype(jnp.float32) * (s_block * jnp.exp(closing[None] - cumulative))[:, :, :, None]).astype(jnp.bfloat16)
        update = jnp.einsum('sghp,sgn->ghpn', block_inputs.astype(jnp.float32), b_block.astype(jnp.float32), precision=highest)
        carried = jnp.exp(closing)[:, :, None, None] * carried + update
        return (carried, outputs)
    start_state = initial.reshape(count_of_groups, per_group, head_width, state_width)
    carried, outputs = lax.scan(advance, start_state, (x_blocks, b_blocks, c_blocks, s_blocks))
    scan_out = outputs.reshape(block_count * block_len, head_count * head_width)
    return (scan_out, carried.reshape(head_count, head_width, state_width))

def gated_norm(scan_out, gate_rows, norm_gain, count_of_groups):
    row_count = scan_out.shape[0]
    gated_rows = scan_out.astype(jnp.float32) * jax.nn.silu(gate_rows.astype(jnp.float32))
    grouped = gated_rows.reshape(row_count, count_of_groups, -1)
    inverse_rms = 1.0 / jnp.sqrt(lax.optimization_barrier(jnp.mean(grouped * grouped, axis=2, keepdims=True)) + epsilon)
    return ((grouped * inverse_rms).reshape(row_count, -1) * norm_gain).astype(jnp.bfloat16)

def slot_table(owners, dest_count, capacity):
    onehot = (owners[:, None] == jnp.arange(dest_count)[None, :]).astype(jnp.int32)
    earlier = jnp.cumsum(onehot, axis=0) - onehot
    slot_rank = lax.optimization_barrier(jnp.sum(earlier * onehot, axis=1))
    slot_hit = (slot_rank[:, None] == jnp.arange(capacity)[None, :]).astype(jnp.float32)
    return onehot.astype(jnp.float32)[:, :, None] * slot_hit[:, None, :]

def reference(x_input, b_input, output_projection_input, step_input, gate_input, kernel_x, kernel_b, kernel_c, step_bias, fading_logarithm, norm_gain, owner_map):
    decay_rate = -jnp.exp(fading_logarithm)
    outputs_all = []
    states_all = []
    for prompt in range(PROMPTS):
        x_conv = causal_filter(x_input[prompt], jnp.zeros((KCONV - 1, x_input.shape[2]), jnp.bfloat16), kernel_x)
        b_conv = causal_filter(b_input[prompt], jnp.zeros((KCONV - 1, b_input.shape[2]), jnp.bfloat16), kernel_b)
        c_conv = causal_filter(output_projection_input[prompt], jnp.zeros((KCONV - 1, output_projection_input.shape[2]), jnp.bfloat16), kernel_c)
        step_size = jax.nn.softplus(step_input[prompt].astype(jnp.float32) + step_bias)
        initial = jnp.zeros((HEADS, HEAD_DIM, STATE), jnp.float32)
        scan_out, closing_state = state_blocks(x_conv, b_conv, c_conv, step_size, decay_rate, initial, STRETCH)
        scan_out = scan_out.astype(jnp.bfloat16)
        outputs_all.append(gated_norm(scan_out, gate_input[prompt], norm_gain, GROUPS))
        owners = owner_map[prompt, :, 0].reshape(HEADS // HB, HB)
        tables = jax.vmap(slot_table, in_axes=(0, None, None))(owners, N_DEC, CAP)
        blocked = closing_state.reshape(HEADS // HB, HB, HEAD_DIM, STATE)
        slots = jnp.einsum('kjer,kjpn->ekrpn', tables, blocked, precision=lax.Precision.HIGHEST)
        states_all.append(slots)
    mixer_output = jnp.stack(outputs_all, axis=0)
    decode_state = jnp.stack(states_all, axis=1)
    return (mixer_output, decode_state)
```

```python
import functools

import jax
import jax.numpy as jnp
from jax import lax
from jax.experimental import pallas as pl
from jax.experimental.pallas import tpu as pltpu
from jax.sharding import PartitionSpec as P

HEAD_DIM = 64
STATE = 256
BLOCK = 256
HB = 4
WIDE = HB * HEAD_DIM
LOG2E = 1.4426950408889634
VMEM = 56 * 1024 * 1024

epsilon = 1e-05
F32 = jnp.float32
BF16 = jnp.bfloat16
HIGHEST = lax.Precision.HIGHEST


def split3(value):
    high = value.astype(BF16)
    rest = value - high.astype(F32)
    middle = rest.astype(BF16)
    low = (rest - middle.astype(F32)).astype(BF16)
    return high, middle, low


def softplus(value):
    return jnp.maximum(value, 0.0) + jnp.log1p(jnp.exp(-jnp.abs(value)))


def silu_of_twice(half):
    return half + half * jnp.tanh(half)


def spread(rows, width, first_head, heads):
    row = lax.broadcasted_iota(jnp.int32, (rows, width), 0)
    channel = lax.broadcasted_iota(jnp.int32, (rows, width), 1)
    head = row % heads
    return (head == first_head + channel // HEAD_DIM).astype(BF16)


def conv(pad_ref, prior, rows, taps):
    count = rows.shape[0]
    pad_ref[0:8, :] = prior
    pad_ref[8 : 8 + count, :] = rows
    taps = taps.astype(F32) * 0.5
    running = taps[0:1] * pad_ref[5 : 5 + count, :]
    for j in range(1, 4):
        running = running + taps[j : j + 1] * pad_ref[5 + j : 5 + j + count, :]
    return silu_of_twice(running).astype(BF16)


def steps_of(step, bias, fading):
    size = softplus(step.astype(F32) + bias)
    decay = -size * jnp.exp(fading)
    count = step.shape[0]
    row = lax.broadcasted_iota(jnp.int32, (count, count), 0)
    col = lax.broadcasted_iota(jnp.int32, (count, count), 1)
    lower = (row >= col).astype(BF16)
    pieces = jnp.concatenate(split3(decay), axis=1)
    sums = jnp.dot(lower, pieces, preferred_element_type=F32)
    heads = step.shape[1]
    cumulative = sums[:, :heads] + sums[:, heads : 2 * heads] + sums[:, 2 * heads :]
    return size, cumulative


def tail_kernel(x_ref, b_ref, c_ref, out_ref):
    at = 0
    for ref in (x_ref, b_ref, c_ref):
        out_ref[:, at : at + ref.shape[1]] = ref[...]
        at += ref.shape[1]


def tail_rows(x, b, c):
    end = x.shape[0] // 16 - 1
    width = x.shape[1] + b.shape[1] + c.shape[1]
    return pl.pallas_call(
        tail_kernel,
        grid=(1,),
        in_specs=[pl.BlockSpec((16, v.shape[1]), lambda i: (end, 0)) for v in (x, b, c)],
        out_specs=pl.BlockSpec((16, width), lambda i: (0, 0)),
        out_shape=jax.ShapeDtypeStruct((16, width), BF16),
        compiler_params=pltpu.CompilerParams(vmem_limit_bytes=VMEM),
        name="tail_rows",
    )(x, b, c)


def update_kernel(
    core_ref, xo_ref, xr_ref, bo_ref, br_ref, so_ref, sr_ref, hx_ref, hb_ref, kx_ref, kb_ref,
    bias_ref, fading_ref, u_ref, first_ref, decay_ref, pad, bo_t, br_t, w_own, w_recv, closing,
):
    i = pl.program_id(0)
    core = core_ref[0]
    heads = so_ref.shape[1]
    even = core == 0

    @pl.when(i == 0)
    def _():
        for step_ref, w_ref, at in ((so_ref, w_own, 0), (sr_ref, w_recv, 1)):
            size, cumulative = steps_of(step_ref[...], bias_ref[...], fading_ref[...])
            last = cumulative[BLOCK - 1 : BLOCK]
            weight = size * jnp.exp(last - cumulative)
            high, middle, _ = split3(weight)
            w_ref[...] = jnp.concatenate([high, middle], axis=1)
            closing[at : at + 1, :] = last

    def pair(own_ref, recv_ref, halo_ref):
        own = own_ref[...].astype(F32)
        recv = recv_ref[...].astype(F32)
        halo = halo_ref[...].astype(F32)[8:]
        prior_own = jnp.where(even, halo, recv[BLOCK - 8 :])
        prior_recv = jnp.where(even, own[BLOCK - 8 :], halo)
        return own, prior_own, recv, prior_recv

    @pl.when(i % 4 == 0)
    def _():
        own, prior_own, recv, prior_recv = pair(bo_ref, br_ref, hb_ref)
        bo_t[...] = conv(pad, prior_own, own, kb_ref[...]).astype(F32).T.astype(BF16)
        br_t[...] = conv(pad, prior_recv, recv, kb_ref[...]).astype(F32).T.astype(BF16)

    first_head = (2 * i + core) * HB
    select = spread(2 * heads, WIDE, first_head, heads)
    own, prior_own, recv, prior_recv = pair(xo_ref, xr_ref, hx_ref)

    def update(rows, prior, w_ref, b_t):
        x_conv = conv(pad, prior, rows, kx_ref[...]).astype(F32)
        weight = jnp.dot(w_ref[...], select, preferred_element_type=F32)
        return jnp.dot(b_t[...], (x_conv * weight).astype(BF16), preferred_element_type=F32)

    u_own = update(own, prior_own, w_own, bo_t)
    u_recv = update(recv, prior_recv, w_recv, br_t)
    last_own = closing[0:1, :]
    last_recv = closing[1:2, :]
    row = lax.broadcasted_iota(jnp.int32, (8, heads), 0)
    logs = jnp.where(row == 0, last_own, jnp.where(row == 1, last_recv, last_own + last_recv))
    pieces = jnp.concatenate(split3(jnp.exp(logs)), axis=1)
    decays = jnp.dot(pieces, spread(3 * heads, WIDE, first_head, heads), preferred_element_type=F32)
    own_factor = jnp.where(even, decays[1:2], 1.0)
    recv_factor = jnp.where(even, 1.0, decays[0:1])
    u_ref[0, 0:STATE, :] = (u_own * own_factor + u_recv * recv_factor).astype(BF16)
    high, middle, low = split3(decays[2:3])
    row = lax.broadcasted_iota(jnp.int32, (16, WIDE), 0)
    u_ref[0, STATE : STATE + 16, :] = jnp.where(
        row == 0,
        high.astype(F32),
        jnp.where(row == 1, middle.astype(F32), jnp.where(row == 2, low.astype(F32), 0.0)),
    ).astype(BF16)
    first_ref[0] = jnp.where(even, u_own, u_recv).astype(BF16)
    decay_ref[0] = jnp.broadcast_to(jnp.where(even, decays[0:1], decays[1:2]), (8, WIDE))


def block_updates(core, x, x_recv, b, b_recv, step, step_recv, halo, kernel_x, kernel_b, bias, fading):
    heads = step.shape[1]
    blocks = x_recv.shape[1] // WIDE // 2
    group_at = x.shape[1] // WIDE
    full = lambda i, c: (0, 0)
    own = lambda i, c: (0, 2 * i + c[0])
    group = lambda i, c: (0, i // 4)
    return pl.pallas_call(
        update_kernel,
        grid_spec=pltpu.PrefetchScalarGridSpec(
            num_scalar_prefetch=1,
            grid=(blocks,),
            in_specs=[
                pl.BlockSpec((BLOCK, WIDE), own),
                pl.BlockSpec((BLOCK, WIDE), own),
                pl.BlockSpec((BLOCK, STATE), group),
                pl.BlockSpec((BLOCK, STATE), group),
                pl.BlockSpec((BLOCK, heads), full),
                pl.BlockSpec((BLOCK, heads), full),
                pl.BlockSpec((16, WIDE), own),
                pl.BlockSpec((16, STATE), lambda i, c: (0, group_at + i // 4)),
                pl.BlockSpec((4, WIDE), own),
                pl.BlockSpec((4, STATE), group),
                pl.BlockSpec((1, heads), full),
                pl.BlockSpec((1, heads), full),
            ],
            out_specs=[
                pl.BlockSpec((1, STATE + 16, WIDE), lambda i, c: (i, 0, 0)),
                pl.BlockSpec((1, STATE, WIDE), lambda i, c: (i, 0, 0)),
                pl.BlockSpec((1, 8, WIDE), lambda i, c: (i, 0, 0)),
            ],
            scratch_shapes=[
                pltpu.VMEM((BLOCK + 8, WIDE), F32),
                pltpu.VMEM((STATE, BLOCK), BF16),
                pltpu.VMEM((STATE, BLOCK), BF16),
                pltpu.VMEM((BLOCK, 2 * heads), BF16),
                pltpu.VMEM((BLOCK, 2 * heads), BF16),
                pltpu.VMEM((8, heads), F32),
            ],
        ),
        out_shape=[
            jax.ShapeDtypeStruct((blocks, STATE + 16, WIDE), BF16),
            jax.ShapeDtypeStruct((blocks, STATE, WIDE), BF16),
            jax.ShapeDtypeStruct((blocks, 8, WIDE), F32),
        ],
        compiler_params=pltpu.CompilerParams(vmem_limit_bytes=VMEM),
        cost_estimate=pl.CostEstimate(flops=600_000_000, bytes_accessed=6_000_000, transcendentals=1_200_000),
        name="block_updates",
    )(core, x, x_recv, b, b_recv, step, step_recv, halo, halo, kernel_x, kernel_b, bias, fading)


def within_kernel(
    core_ref, x_ref, gate_ref, b_ref, c_ref, step_ref, hx_ref, hb_ref, hc_ref, tx_ref, tb_ref, tc_ref,
    kx_ref, kb_ref, kc_ref, bias_ref, fading_ref, a_ref, g_ref, cc_ref, pad, pieces, cum_t, scores, cross, x_step,
):
    k = pl.program_id(0)
    even = core_ref[0] == 0

    def filtered(rows_ref, halo_ref, tail_ref, taps_ref):
        prior = jnp.where(even, halo_ref[...].astype(F32), tail_ref[...].astype(F32))[8:]
        return conv(pad, prior, rows_ref[...].astype(F32), taps_ref[...])

    heads = step_ref.shape[1]
    half = BLOCK // 2

    @pl.when(k == 0)
    def _():
        size, cumulative = steps_of(step_ref[...], bias_ref[...], fading_ref[...])
        cumulative = cumulative * LOG2E
        pieces[0] = jnp.concatenate(split3(cumulative), axis=1)
        pieces[1] = jnp.concatenate(split3(size), axis=1)
        turned = cumulative.T
        for n in range(heads // HB):
            cum_t[n, 0:HB, :] = turned[n * HB : (n + 1) * HB]

    @pl.when(k % 8 == 0)
    def _():
        b_conv = filtered(b_ref, hb_ref, tb_ref, kb_ref)
        c_conv = filtered(c_ref, hc_ref, tc_ref, kc_ref)
        cc_ref[...] = c_conv
        products = lax.dot_general(
            c_conv, b_conv, (((1,), (1,)), ((), ())), preferred_element_type=F32
        )
        row = lax.broadcasted_iota(jnp.int32, (half, half), 0)
        col = lax.broadcasted_iota(jnp.int32, (half, half), 1)
        for a in range(2):
            at = slice(a * half, (a + 1) * half)
            scores[at, :] = jnp.where(row >= col, products[at, at], 0.0)
        cross[...] = products[half:, :half].astype(BF16)

    select = spread(3 * heads, WIDE, k * HB, heads)
    cum_wide = jnp.dot(pieces[0], select, preferred_element_type=F32)
    step_wide = jnp.dot(pieces[1], select, preferred_element_type=F32)
    x_conv = filtered(x_ref, hx_ref, tx_ref, kx_ref).astype(F32)
    stepped = x_conv * step_wide
    x_step[...] = stepped.astype(BF16)
    lines = cum_t[k]
    middle = cum_wide[half - 1 : half]
    scaled = (stepped[:half] * jnp.exp2(middle - cum_wide[:half])).astype(BF16)
    late = jnp.dot(cross[...], scaled, preferred_element_type=F32)
    late = late * jnp.exp2(cum_wide[half:] - middle)
    gate = silu_of_twice(gate_ref[...].astype(F32) * 0.5)
    g_ref[...] = (jnp.exp2(cum_wide) * gate).astype(BF16)
    for a in range(2):
        at = slice(a * half, (a + 1) * half)
        parts = []
        for j in range(HB):
            column = cum_wide[at, j * HEAD_DIM : j * HEAD_DIM + 1]
            line = lines[j : j + 1, at]
            weights = scores[at, :] * jnp.exp2(jnp.minimum(column - line, 0.0))
            parts.append(
                jnp.dot(
                    weights.astype(BF16),
                    x_step[at, j * HEAD_DIM : (j + 1) * HEAD_DIM],
                    preferred_element_type=F32,
                )
            )
        inside = jnp.concatenate(parts, axis=1)
        if a == 1:
            inside = inside + late
        a_ref[at, :] = (inside * gate[at]).astype(BF16)


def within_block(core, x, gate, b, c, step, halo, x_recv, b_recv, c_recv, kernel_x, kernel_b, kernel_c, bias, fading):
    heads = step.shape[1]
    blocks = x.shape[1] // WIDE
    groups = b.shape[1] // STATE
    per_group = blocks // groups
    end = BLOCK // 16 - 1
    full = lambda k, s: (0, 0)
    group = lambda k, s: (0, k // per_group)
    one = lambda k, s: (0, k)
    return pl.pallas_call(
        within_kernel,
        grid_spec=pltpu.PrefetchScalarGridSpec(
            num_scalar_prefetch=1,
            grid=(blocks,),
            in_specs=[
                pl.BlockSpec((BLOCK, WIDE), one),
                pl.BlockSpec((BLOCK, WIDE), one),
                pl.BlockSpec((BLOCK, STATE), group),
                pl.BlockSpec((BLOCK, STATE), group),
                pl.BlockSpec((BLOCK, heads), full),
                pl.BlockSpec((16, WIDE), one),
                pl.BlockSpec((16, STATE), lambda k, s: (0, blocks + k // per_group)),
                pl.BlockSpec((16, STATE), lambda k, s: (0, blocks + groups + k // per_group)),
                pl.BlockSpec((16, WIDE), lambda k, s: (end, k)),
                pl.BlockSpec((16, STATE), lambda k, s: (end, k // per_group)),
                pl.BlockSpec((16, STATE), lambda k, s: (end, k // per_group)),
                pl.BlockSpec((4, WIDE), one),
                pl.BlockSpec((4, STATE), group),
                pl.BlockSpec((4, STATE), group),
                pl.BlockSpec((1, heads), full),
                pl.BlockSpec((1, heads), full),
            ],
            out_specs=[
                pl.BlockSpec((BLOCK, WIDE), one),
                pl.BlockSpec((BLOCK, WIDE), one),
                pl.BlockSpec((BLOCK, STATE), group),
            ],
            scratch_shapes=[
                pltpu.VMEM((BLOCK + 8, WIDE), F32),
                pltpu.VMEM((2, BLOCK, 3 * heads), BF16),
                pltpu.VMEM((heads // HB, 8, BLOCK), F32),
                pltpu.VMEM((BLOCK, BLOCK // 2), F32),
                pltpu.VMEM((BLOCK // 2, BLOCK // 2), BF16),
                pltpu.VMEM((BLOCK, WIDE), BF16),
            ],
        ),
        out_shape=[
            jax.ShapeDtypeStruct(x.shape, BF16),
            jax.ShapeDtypeStruct(x.shape, BF16),
            jax.ShapeDtypeStruct(c.shape, BF16),
        ],
        compiler_params=pltpu.CompilerParams(vmem_limit_bytes=VMEM),
        cost_estimate=pl.CostEstimate(flops=8_000_000_000, bytes_accessed=12_000_000, transcendentals=6_000_000),
        name="within_block",
    )(
        core, x, gate, b, c, step, halo, halo, halo, x_recv, b_recv, c_recv, kernel_x, kernel_b, kernel_c,
        bias, fading,
    )


def scan_kernel(gathered_ref, decay_ref, _, starts_ref, final_ref):
    state = jnp.zeros(final_ref.shape, F32)
    for n in range(gathered_ref.shape[0]):
        starts_ref[n] = state.astype(BF16)
        decay = jnp.sum(decay_ref[n].astype(F32), axis=0, keepdims=True)
        state = state * decay + gathered_ref[n].astype(F32)
    final_ref[...] = state


def scan_states(gathered, after):
    chips = gathered.shape[0]
    rows = STATE // 4
    return pl.pallas_call(
        scan_kernel,
        grid=(4,),
        in_specs=[
            pl.BlockSpec((chips, rows, WIDE), lambda r: (0, r, 0)),
            pl.BlockSpec((chips, 16, WIDE), lambda r: (0, STATE // 16, 0)),
            pl.BlockSpec(memory_space=pl.ANY),
        ],
        out_specs=[
            pl.BlockSpec((chips, rows, WIDE), lambda r: (0, r, 0)),
            pl.BlockSpec((rows, WIDE), lambda r: (r, 0)),
        ],
        out_shape=[
            jax.ShapeDtypeStruct((chips, STATE, WIDE), BF16),
            jax.ShapeDtypeStruct((STATE, WIDE), F32),
        ],
        compiler_params=pltpu.CompilerParams(vmem_limit_bytes=VMEM),
        cost_estimate=pl.CostEstimate(flops=2_000_000, bytes_accessed=2_500_000, transcendentals=0),
        name="scan_states",
    )(gathered, gathered, after)


def start_kernel(core_ref, start_ref, first_ref, decay_ref, _, keep_ref, send_ref):
    even = core_ref[0] == 0
    start = start_ref[...].astype(F32)
    later = start * decay_ref[:, 0:1, :] + first_ref[...].astype(F32)
    keep_ref[...] = jnp.where(even, start, later).astype(BF16)
    send_ref[...] = jnp.where(even, later, start).astype(BF16)


def block_starts(core, chip_start, first_update, first_decay, after):
    blocks = chip_start.shape[0]
    part = blocks // 2
    one = lambda i, c: (i, 0, 0)
    shape = jax.ShapeDtypeStruct(chip_start.shape, BF16)
    return pl.pallas_call(
        start_kernel,
        grid_spec=pltpu.PrefetchScalarGridSpec(
            num_scalar_prefetch=1,
            grid=(blocks // part,),
            in_specs=[
                pl.BlockSpec((part, STATE, WIDE), one),
                pl.BlockSpec((part, STATE, WIDE), one),
                pl.BlockSpec((part, 8, WIDE), one),
                pl.BlockSpec(memory_space=pl.ANY),
            ],
            out_specs=[pl.BlockSpec((part, STATE, WIDE), one)] * 2,
        ),
        out_shape=[shape, shape],
        compiler_params=pltpu.CompilerParams(vmem_limit_bytes=VMEM),
        cost_estimate=pl.CostEstimate(flops=2_000_000, bytes_accessed=4_500_000, transcendentals=0),
        name="block_starts",
    )(core, chip_start, first_update, first_decay, after)


def finish_kernel(core_ref, a_ref, g_ref, cc_ref, keep_ref, recv_ref, gain_ref, out_ref, y_ref):
    core = core_ref[0]
    rows, width = a_ref.shape
    total = jnp.zeros((rows, 1), F32)
    c_conv = cc_ref[...]
    for j in range(keep_ref.shape[0]):
        for state_ref, parity in ((keep_ref, core), (recv_ref, 1 - core)):
            at = pl.ds(pl.multiple_of((2 * j + parity) * WIDE, WIDE), WIDE)
            carried = jnp.dot(c_conv, state_ref[j], preferred_element_type=F32)
            y = a_ref[:, at].astype(F32) + carried * g_ref[:, at].astype(F32)
            y_ref[:, at] = y
            total = total + jnp.sum(y * y, axis=1, keepdims=True)
    inverse = 1.0 / jnp.sqrt(total / width + epsilon)
    out_ref[...] = (y_ref[...] * inverse * gain_ref[...]).astype(BF16)


def finish(core, a, g, cc, keep, recv, gain):
    tokens, channels = a.shape
    groups = cc.shape[1] // STATE
    width = channels // groups
    per_group = keep.shape[0] // groups
    rows = tokens // 2
    return pl.pallas_call(
        finish_kernel,
        grid_spec=pltpu.PrefetchScalarGridSpec(
            num_scalar_prefetch=1,
            grid=(groups, 2),
            in_specs=[
                pl.BlockSpec((rows, width), lambda n, r, c: (r, n)),
                pl.BlockSpec((rows, width), lambda n, r, c: (r, n)),
                pl.BlockSpec((rows, STATE), lambda n, r, c: (r, n)),
                pl.BlockSpec((per_group, STATE, WIDE), lambda n, r, c: (n, 0, 0)),
                pl.BlockSpec((per_group, STATE, WIDE), lambda n, r, c: (n, 0, 0)),
                pl.BlockSpec((1, width), lambda n, r, c: (0, n)),
            ],
            out_specs=pl.BlockSpec((rows, width), lambda n, r, c: (r, n)),
            scratch_shapes=[pltpu.VMEM((rows, width), F32)],
        ),
        out_shape=jax.ShapeDtypeStruct((tokens, channels), BF16),
        compiler_params=pltpu.CompilerParams(vmem_limit_bytes=VMEM),
        cost_estimate=pl.CostEstimate(flops=600_000_000, bytes_accessed=9_000_000, transcendentals=1000),
        name="finish",
    )(core, a, g, cc, keep, recv, gain)


def slot_table(owners, dest_count, capacity):
    onehot = (owners[:, None] == jnp.arange(dest_count)[None, :]).astype(jnp.int32)
    earlier = jnp.cumsum(onehot, axis=0) - onehot
    slot_rank = jnp.sum(earlier * onehot, axis=1)
    slot_hit = (slot_rank[:, None] == jnp.arange(capacity)[None, :]).astype(F32)
    return onehot.astype(F32)[:, :, None] * slot_hit[:, None, :]


def local(
    x_input, b_input, output_projection_input, step_input, gate_input, kernel_x, kernel_b, kernel_c,
    step_bias, fading_logarithm, norm_gain, owner_map,
):
    ctx_count = lax.axis_size("ctx")
    ctx_rank = lax.axis_index("ctx")
    dec_count = lax.axis_size("dec")
    dec_rank = lax.axis_index("dec")
    core = ctx_rank % 2
    core_arg = core.astype(jnp.int32).reshape(1)
    x = x_input[0]
    b = b_input[0]
    c = output_projection_input[0]
    step = step_input[0]
    bias = step_bias.reshape(1, -1)
    fading = fading_logarithm.reshape(1, -1)

    swap = [(i, i ^ 1) for i in range(ctx_count)]
    tail = tail_rows(x, b, c)
    x_recv, b_recv, step_recv, c_recv = (
        lax.ppermute(x, "ctx", swap),
        lax.ppermute(b, "ctx", swap),
        lax.ppermute(step, "ctx", swap),
        lax.ppermute(c, "ctx", swap),
    )
    from_even = lax.ppermute(tail, "ctx", [(i, i + 1) for i in range(1, ctx_count - 1, 2)])
    from_odd = lax.ppermute(tail, "ctx", [(i, i + 2) for i in range(1, ctx_count - 2, 2)])
    halo_chip = jnp.where(core == 0, from_even, from_odd)

    updates, first_update, first_decay = block_updates(
        core_arg, x, x_recv, b, b_recv, step, step_recv, halo_chip, kernel_x, kernel_b, bias, fading
    )
    same_core = [[2 * i + j for i in range(ctx_count // 2)] for j in range(2)]
    gathered = lax.all_to_all(updates, "ctx", 0, 0, axis_index_groups=same_core, tiled=True)
    a, g, cc = within_block(
        core_arg, x, gate_input[0], b, c, step, from_even, x_recv, b_recv, c_recv,
        kernel_x, kernel_b, kernel_c, bias, fading,
    )
    starts, state = scan_states(gathered, cc)
    chip_start = lax.all_to_all(starts, "ctx", 0, 0, axis_index_groups=same_core, tiled=True)

    owners = lax.dynamic_slice_in_dim(owner_map[0, :, 0], ctx_rank * HB, HB)
    table = slot_table(owners, dec_count, 2)
    finals = state.T.reshape(HB, HEAD_DIM, STATE)
    outgoing = jnp.sum(table[:, :, :, None, None] * finals[:, None, None], axis=0)
    arrived = jnp.zeros(outgoing.shape, F32)
    for d in range(dec_count):
        piece = lax.dynamic_index_in_dim(outgoing, dec_rank ^ d, 0, keepdims=False)
        if d:
            piece = lax.ppermute(piece, "dec", [(i, i ^ d) for i in range(dec_count)])
        arrived = lax.dynamic_update_index_in_dim(arrived, piece, dec_rank ^ d, 0)

    keep, send = block_starts(core_arg, chip_start, first_update, first_decay, arrived)
    recv = lax.ppermute(send, "ctx", swap)
    mixer_rows = finish(core_arg, a, g, cc, keep, recv, norm_gain.reshape(1, -1))
    return (mixer_rows[None], arrived[None, :, None])


def solution(mesh):
    return jax.shard_map(
        local,
        mesh=mesh,
        in_specs=(
            P("dec", "ctx", "tp"),
            P("dec", "ctx", "tp"),
            P("dec", "ctx", "tp"),
            P("dec", "ctx", "tp"),
            P("dec", "ctx", "tp"),
            P(None, "tp"),
            P(None, "tp"),
            P(None, "tp"),
            P("tp"),
            P("tp"),
            P("tp"),
            P("dec", "tp", None),
        ),
        out_specs=(P("dec", "ctx", "tp"), P("dec", None, ("tp", "ctx"), None, None, None)),
        check_vma=False,
    )
```

```python
import functools

import jax
import jax.numpy as jnp
from jax import lax
from jax.experimental import pallas as pl
from jax.experimental.pallas import tpu as pltpu
from jax.sharding import PartitionSpec as P

HEAD_DIM = 64
STATE = 256
BLOCK = 256
HB = 4
WIDE = HB * HEAD_DIM
LOG2E = 1.4426950408889634
VMEM = 40 * 1024 * 1024
SMALL = 12 * 1024 * 1024
IN_VMEM = pl.BlockSpec(memory_space=pltpu.VMEM)
IN_HBM = pl.BlockSpec(memory_space=pl.ANY)


def hbm(value):
    return pltpu.with_memory_space_constraint(value, pltpu.HBM)


def vmem(value):
    return pltpu.with_memory_space_constraint(value, pltpu.VMEM)

epsilon = 1e-05
F32 = jnp.float32
BF16 = jnp.bfloat16
HIGHEST = lax.Precision.HIGHEST


def split3(value):
    high = value.astype(BF16)
    rest = value - high.astype(F32)
    middle = rest.astype(BF16)
    low = (rest - middle.astype(F32)).astype(BF16)
    return high, middle, low


def softplus(value):
    return jnp.maximum(value, 0.0) + jnp.log1p(jnp.exp(-jnp.abs(value)))


def silu_of_twice(half):
    return half + half * jnp.tanh(half)


def spread(rows, width, first_head, heads):
    row = lax.broadcasted_iota(jnp.int32, (rows, width), 0)
    channel = lax.broadcasted_iota(jnp.int32, (rows, width), 1)
    head = row % heads
    return (head == first_head + channel // HEAD_DIM).astype(BF16)


def conv(pad_ref, prior, rows, taps):
    count = rows.shape[0]
    pad_ref[0:8, :] = prior
    pad_ref[8 : 8 + count, :] = rows
    taps = taps.astype(F32) * 0.5
    running = taps[0:1] * pad_ref[5 : 5 + count, :]
    for j in range(1, 4):
        running = running + taps[j : j + 1] * pad_ref[5 + j : 5 + j + count, :]
    return silu_of_twice(running).astype(BF16)


def edge_sums(prior, rows, taps):
    both = jnp.concatenate([prior, rows], axis=0)
    taps = taps.astype(F32) * 0.5
    running = taps[0:1] * both[5:13]
    for j in range(1, 4):
        running = running + taps[j : j + 1] * both[5 + j : 13 + j]
    return running


def steps_of(step, bias, fading):
    size = softplus(step.astype(F32) + bias)
    decay = -size * jnp.exp(fading)
    count = step.shape[0]
    row = lax.broadcasted_iota(jnp.int32, (count, count), 0)
    col = lax.broadcasted_iota(jnp.int32, (count, count), 1)
    lower = (row >= col).astype(BF16)
    pieces = jnp.concatenate(split3(decay), axis=1)
    sums = jnp.dot(lower, pieces, preferred_element_type=F32)
    heads = step.shape[1]
    cumulative = sums[:, :heads] + sums[:, heads : 2 * heads] + sums[:, 2 * heads :]
    return size, cumulative


def lanes(block, width=WIDE):
    return pl.ds(pl.multiple_of(block * width, width), width)


def weights_of(step, bias, fading):
    size, cumulative = steps_of(step, bias, fading)
    last = cumulative[-1:]
    high, middle, _ = split3(size * jnp.exp(last - cumulative))
    return jnp.concatenate([high, middle], axis=1), last


def whole(value):
    return pl.BlockSpec(value.shape, lambda *_: (0,) * value.ndim)


def own_kernel(
    core_ref, x_ref, b_ref, ct_ref, step_ref, kx_ref, kb_ref, bias_ref, fading_ref,
    u_ref, first_weight_ref, closing_ref, tail_ref, pad, weight,
):
    n = pl.program_id(0)
    core = core_ref[0]
    heads = step_ref.shape[1]
    per_group = u_ref.shape[0] // 2
    end = slice(BLOCK - 16, BLOCK)
    x_width, b_width = x_ref.shape[1], b_ref.shape[1]
    tail_ref[:, lanes(n, x_width)] = x_ref[end, :]
    tail_ref[:, lanes(2 * x_width // b_width + n, b_width)] = b_ref[end, :]
    tail_ref[:, 2 * (x_width + b_width) :] = ct_ref[...]

    @pl.when(n == 0)
    def _():
        value, last = weights_of(step_ref[...], bias_ref[...], fading_ref[...])
        first_weight_ref[...] = value[0:16]
        closing_ref[...] = jnp.broadcast_to(last, (8, heads))
        row = lax.broadcasted_iota(jnp.int32, value.shape, 0)
        weight[...] = jnp.where(row < 8, 0.0, value.astype(F32)).astype(BF16)

    none = jnp.zeros((8, STATE), F32)
    b_t = conv(pad.at[0], none, b_ref[...].astype(F32), kb_ref[...]).astype(F32).T.astype(BF16)
    for j in range(per_group):
        block = 2 * j + core
        at = lanes(block)
        x_conv = conv(pad.at[j % 2], none, x_ref[:, at].astype(F32), kx_ref[:, at]).astype(F32)
        select = spread(2 * heads, WIDE, (2 * per_group * n + block) * HB, heads)
        inputs = x_conv * jnp.dot(weight[...], select, preferred_element_type=F32)
        u_ref[n * per_group + j] = jnp.dot(b_t, inputs.astype(BF16), preferred_element_type=F32)


def own_updates(core, x, b, c, step, kernel_x, kernel_b, bias, fading):
    heads = step.shape[1]
    groups = b.shape[1] // STATE
    width = x.shape[1] // groups
    blocks = x.shape[1] // WIDE // 2
    one = lambda n, c: (0, n)
    return pl.pallas_call(
        own_kernel,
        grid_spec=pltpu.PrefetchScalarGridSpec(
            num_scalar_prefetch=1,
            grid=(groups,),
            in_specs=[
                pl.BlockSpec((BLOCK, width), one),
                pl.BlockSpec((BLOCK, STATE), one),
                pl.BlockSpec((16, c.shape[1]), lambda n, s: (BLOCK // 16 - 1, 0)),
                whole(step),
                pl.BlockSpec((4, width), one),
                pl.BlockSpec((4, STATE), one),
                whole(bias),
                whole(fading),
            ],
            out_specs=[IN_VMEM, IN_VMEM, IN_VMEM, IN_VMEM],
            scratch_shapes=[
                pltpu.VMEM((2, BLOCK + 8, WIDE), F32),
                pltpu.VMEM((BLOCK, 2 * heads), BF16),
            ],
        ),
        out_shape=[
            pltpu.VMEM((blocks, STATE, WIDE), F32),
            pltpu.VMEM((16, 2 * heads), BF16),
            pltpu.VMEM((8, heads), F32),
            pltpu.VMEM((16, x.shape[1] + b.shape[1] + c.shape[1]), BF16),
        ],
        compiler_params=pltpu.CompilerParams(vmem_limit_bytes=VMEM),
        cost_estimate=pl.CostEstimate(flops=300_000_000, bytes_accessed=10_000_000, transcendentals=600_000),
        name="own_updates",
    )(core, hbm(x), hbm(b), hbm(c), hbm(step), hbm(kernel_x), hbm(kernel_b), hbm(bias), hbm(fading))


def chip_kernel(
    core_ref, u_own_ref, first_weight_ref, closing_ref, xh_ref, xt_ref, bh_ref, bt_ref, xr_ref, br_ref,
    sr_ref, kx_ref, kb_ref, bias_ref, fading_ref,
    u_ref, first_ref, decay_ref, edge_ref, pad, small, extra, weight, weight_first, values,
):
    n = pl.program_id(0)
    core = core_ref[0]
    even = core == 0
    heads = sr_ref.shape[1]
    per_group = u_ref.shape[0]
    head8 = slice(0, 8)
    tail8 = slice(8, 16)

    @pl.when(n == 0)
    def _():
        value, last = weights_of(sr_ref[...], bias_ref[...], fading_ref[...])
        row = lax.broadcasted_iota(jnp.int32, value.shape, 0)
        weight[...] = jnp.where((row < 3) & jnp.logical_not(even), 0.0, value.astype(F32)).astype(BF16)
        mine = first_weight_ref[...].astype(F32)
        row = lax.broadcasted_iota(jnp.int32, mine.shape, 0)
        dropped = (row >= 8) | ((row < 3) & even)
        weight_first[...] = jnp.where(dropped, 0.0, mine).astype(BF16)
        edge = jnp.where(even, mine, value[0:16].astype(F32))
        edge = edge[:, :heads] + edge[:, heads:]
        own = jnp.exp(closing_ref[0:1, :])
        other = jnp.exp(last)
        values[0:1, :] = own
        values[1:2, :] = other
        values[2:3, :] = jnp.exp(closing_ref[0:1, :] + last)
        values[3:6, :] = edge[0:3] * jnp.where(even, other, own)
        values[6:9, :] = edge[0:3]
        values[9:16, :] = jnp.zeros((7, heads), F32)

    def edges(own_head, own_end, recv_head, recv_end, taps):
        none = jnp.zeros(own_head.shape, F32)
        first = edge_sums(none, jnp.where(even, own_head, recv_head), taps)
        last = edge_sums(jnp.where(even, recv_end, own_end), none, taps)
        return jnp.where(even, none, recv_end), jnp.where(even, own_end, none), first, last

    def rows_of(ref, rows, at):
        return ref[rows, at].astype(F32)

    end = slice(BLOCK - 16, BLOCK)
    at = lanes(n, STATE)
    everything = slice(None)
    prior_own, prior_recv, b_first, b_last = edges(
        rows_of(bh_ref, slice(0, 16), everything)[head8],
        rows_of(bt_ref, slice(0, 16), everything)[tail8],
        rows_of(br_ref, slice(0, 16), at)[head8],
        rows_of(br_ref, end, at)[tail8],
        kb_ref[...],
    )
    b_own = conv(small.at[0], prior_own, bh_ref[...].astype(F32), kb_ref[...])
    b_recv = conv(pad.at[0], prior_recv, br_ref[:, at].astype(F32), kb_ref[...])
    b_own = b_own.astype(F32).T.astype(BF16)
    b_recv = b_recv.astype(F32).T.astype(BF16)
    pieces = jnp.concatenate(split3(values[...]), axis=1)
    for j in range(per_group):
        block = 2 * j + core
        head = (2 * per_group * n + block) * HB
        here = lanes(block)
        at = lanes(2 * per_group * n + block)
        taps = kx_ref[:, here]
        select = spread(2 * heads, WIDE, head, heads)
        prior_own, prior_recv, x_first, x_last = edges(
            rows_of(xh_ref, slice(0, 16), here)[head8],
            rows_of(xt_ref, slice(0, 16), here)[tail8],
            rows_of(xr_ref, slice(0, 16), at)[head8],
            rows_of(xr_ref, end, at)[tail8],
            taps,
        )
        x_own = conv(small.at[j % 2], prior_own, xh_ref[:, here].astype(F32), taps).astype(F32)
        x_own = x_own * jnp.dot(weight_first[...], select, preferred_element_type=F32)
        x_conv = conv(pad.at[j % 2], prior_recv, xr_ref[:, at].astype(F32), taps).astype(F32)
        inputs = x_conv * jnp.dot(weight[...], select, preferred_element_type=F32)
        u_recv = jnp.dot(b_recv, inputs.astype(BF16), preferred_element_type=F32)
        u_own = u_own_ref[n * per_group + j] + jnp.dot(
            b_own, x_own.astype(BF16), preferred_element_type=F32
        )
        wide = jnp.dot(pieces, spread(3 * heads, WIDE, head, heads), preferred_element_type=F32)
        own_factor = jnp.where(even, wide[1:2], 1.0)
        recv_factor = jnp.where(even, 1.0, wide[0:1])
        u_ref[j, 0:STATE, :] = (u_own * own_factor + u_recv * recv_factor).astype(BF16)
        first_ref[j] = jnp.where(even, u_own, u_recv).astype(BF16)
        decay_ref[j] = jnp.broadcast_to(jnp.where(even, wide[0:1], wide[1:2]), (8, WIDE))
        high, middle, low = split3(wide[2:3])
        place = lax.broadcasted_iota(jnp.int32, (1, WIDE), 1) % HEAD_DIM // 8
        packed = jnp.zeros((1, WIDE), F32)
        for q, value in enumerate((high, middle, low, wide[3:4], wide[4:5], wide[5:6])):
            packed = jnp.where(place == q, value.astype(F32), packed)
        extra[0:1, :] = packed
        extra[1:4, :] = x_first[0:3]
        extra[4:7, :] = x_last[0:3]
        extra[7:10, :] = b_first[0:3]
        extra[10:13, :] = b_last[0:3]
        extra[13:16, :] = jnp.zeros((3, WIDE), F32)
        u_ref[j, STATE : STATE + 16, :] = extra[...].astype(BF16)
        edge_ref[j, 0:3, :] = x_first[0:3]
        edge_ref[j, 3:6, :] = b_first[0:3]
        edge_ref[j, 6:9, :] = wide[6:9]
        edge_ref[j, 9:16, :] = jnp.zeros((7, WIDE), F32)


def chip_updates(core, own, x, b, x_recv, b_recv, step_recv, kernel_x, kernel_b, bias, fading):
    u_own, first_weight, closing = own
    heads = step_recv.shape[1]
    groups = b.shape[1] // STATE
    width = x.shape[1] // groups
    blocks = x.shape[1] // WIDE // 2
    per_group = blocks // groups
    end = BLOCK // 16 - 1
    one = lambda n, c: (0, n)
    tail = lambda n, c: (end, n)
    out = lambda n, c: (n, 0, 0)
    return pl.pallas_call(
        chip_kernel,
        grid_spec=pltpu.PrefetchScalarGridSpec(
            num_scalar_prefetch=1,
            grid=(groups,),
            in_specs=[
                IN_VMEM,
                IN_VMEM,
                IN_VMEM,
                pl.BlockSpec((16, width), one),
                pl.BlockSpec((16, width), tail),
                pl.BlockSpec((16, STATE), one),
                pl.BlockSpec((16, STATE), tail),
                IN_VMEM,
                IN_VMEM,
                IN_VMEM,
                pl.BlockSpec((4, width), one),
                pl.BlockSpec((4, STATE), one),
                whole(bias),
                whole(fading),
            ],
            out_specs=[
                pl.BlockSpec((per_group, STATE + 16, WIDE), out),
                pl.BlockSpec((per_group, STATE, WIDE), out),
                pl.BlockSpec((per_group, 8, WIDE), out),
                pl.BlockSpec((per_group, 16, WIDE), out),
            ],
            scratch_shapes=[
                pltpu.VMEM((2, BLOCK + 8, WIDE), F32),
                pltpu.VMEM((2, 24, WIDE), F32),
                pltpu.VMEM((16, WIDE), F32),
                pltpu.VMEM((BLOCK, 2 * heads), BF16),
                pltpu.VMEM((16, 2 * heads), BF16),
                pltpu.VMEM((16, heads), F32),
            ],
        ),
        out_shape=[
            pltpu.HBM((blocks, STATE + 16, WIDE), BF16),
            pltpu.HBM((blocks, STATE, WIDE), BF16),
            pltpu.HBM((blocks, 8, WIDE), F32),
            pltpu.HBM((blocks, 16, WIDE), F32),
        ],
        compiler_params=pltpu.CompilerParams(vmem_limit_bytes=VMEM),
        cost_estimate=pl.CostEstimate(flops=300_000_000, bytes_accessed=10_000_000, transcendentals=600_000),
        name="chip_updates",
    )(
        core, vmem(u_own), vmem(first_weight), vmem(closing), hbm(x), hbm(x), hbm(b), hbm(b), vmem(x_recv),
        vmem(b_recv), vmem(step_recv), hbm(kernel_x), hbm(kernel_b), hbm(bias), hbm(fading),
    )


def edge_kernel(core_ref, first_ref, edge_ref, he_ref, ho_ref, kx_ref, kb_ref, out_ref):
    n = pl.program_id(0)
    core = core_ref[0]
    even = core == 0
    per_group = first_ref.shape[0]
    blocks = 2 * per_group * pl.num_programs(0)
    none = jnp.zeros((8, WIDE), F32)
    row = lax.broadcasted_iota(jnp.int32, (16, WIDE), 0)

    def from_halo(at, taps):
        halo = jnp.where(even, he_ref[:, at].astype(F32), ho_ref[:, at].astype(F32))[8:]
        return edge_sums(halo, none, taps)[0:3]

    b_sums = from_halo(lanes(blocks + n, STATE), kb_ref[...])
    for j in range(per_group):
        block = 2 * j + core
        x_sums = from_halo(lanes(2 * per_group * n + block), kx_ref[:, lanes(block)])
        rows = edge_ref[j]
        x_conv = silu_of_twice(rows[0:3] + x_sums).astype(BF16).astype(F32)
        b_conv = silu_of_twice(rows[3:6] + b_sums)
        inputs = x_conv * rows[6:9]
        pad = jnp.zeros((13, WIDE), F32)
        inputs = jnp.concatenate([inputs, pad], axis=0).astype(BF16)
        b_conv = jnp.concatenate([b_conv, pad], axis=0).astype(BF16)
        term = lax.dot_general(b_conv, inputs, (((0,), (0,)), ((), ())), preferred_element_type=F32)
        out_ref[j] = (first_ref[j].astype(F32) + term).astype(BF16)


def whole_first(core, first, edge, halo_even, halo_odd, kernel_x, kernel_b):
    groups = kernel_b.shape[1] // STATE
    per_group = first.shape[0] // groups
    width = kernel_x.shape[1] // groups
    out = lambda n, c: (n, 0, 0)
    one = lambda n, c: (0, n)
    return pl.pallas_call(
        edge_kernel,
        grid_spec=pltpu.PrefetchScalarGridSpec(
            num_scalar_prefetch=1,
            grid=(groups,),
            in_specs=[
                pl.BlockSpec((per_group, STATE, WIDE), out),
                pl.BlockSpec((per_group, 16, WIDE), out),
                IN_VMEM,
                IN_VMEM,
                pl.BlockSpec((4, width), one),
                pl.BlockSpec((4, STATE), one),
            ],
            out_specs=pl.BlockSpec((per_group, STATE, WIDE), out),
        ),
        out_shape=pltpu.HBM(first.shape, BF16),
        compiler_params=pltpu.CompilerParams(vmem_limit_bytes=SMALL),
        cost_estimate=pl.CostEstimate(flops=30_000_000, bytes_accessed=3_000_000, transcendentals=10_000),
        name="whole_first",
    )(core, hbm(first), hbm(edge), vmem(halo_even), vmem(halo_odd), hbm(kernel_x), hbm(kernel_b))


def within_kernel(
    core_ref, x_ref, gate_ref, b_ref, c_ref, step_ref, halo_ref, tx_ref, tb_ref, tc_ref,
    kx_ref, kb_ref, kc_ref, bias_ref, fading_ref, a_ref, g_ref, cc_ref, pad, pieces, cum_t, scores, cross, x_step,
):
    k = pl.program_id(0)
    even = core_ref[0] == 0
    heads = step_ref.shape[1]
    half = BLOCK // 2
    steps = pl.num_programs(0)
    blocks = x_ref.shape[1] // WIDE
    group = k // (steps // 2)
    end = slice(BLOCK - 16, BLOCK)

    def prior(halo_at, tail_ref, at):
        halo = halo_ref[:, lanes(halo_at)].astype(F32)
        return jnp.where(even, halo, tail_ref[end, lanes(at)].astype(F32))[8:]

    @pl.when(k == 0)
    def _():
        size, cumulative = steps_of(step_ref[...], bias_ref[...], fading_ref[...])
        cumulative = cumulative * LOG2E
        pieces[0] = jnp.concatenate(split3(cumulative), axis=1)
        pieces[1] = jnp.concatenate(split3(size), axis=1)
        turned = cumulative.T
        for n in range(heads // HB):
            cum_t[n, 0:HB, :] = turned[n * HB : (n + 1) * HB]

    @pl.when(k % (steps // 2) == 0)
    def _():
        in_halo = steps * blocks + group
        b_conv = conv(pad.at[0], prior(in_halo, tb_ref, group), b_ref[...].astype(F32), kb_ref[...])
        c_conv = conv(pad.at[1], prior(in_halo + 2, tc_ref, group), c_ref[...].astype(F32), kc_ref[...])
        cc_ref[...] = c_conv
        products = lax.dot_general(
            c_conv, b_conv, (((1,), (1,)), ((), ())), preferred_element_type=F32
        )
        row = lax.broadcasted_iota(jnp.int32, (half, half), 0)
        col = lax.broadcasted_iota(jnp.int32, (half, half), 1)
        for a in range(2):
            at = slice(a * half, (a + 1) * half)
            scores[at, :] = jnp.where(row >= col, products[at, at], 0.0)
        cross[...] = products[half:, :half].astype(BF16)

    for m in range(blocks):
        block = k * blocks + m
        here = slice(m * WIDE, (m + 1) * WIDE)
        select = spread(3 * heads, WIDE, block * HB, heads)
        cum_wide = jnp.dot(pieces[0], select, preferred_element_type=F32)
        step_wide = jnp.dot(pieces[1], select, preferred_element_type=F32)
        rows = x_ref[:, here].astype(F32)
        x_conv = conv(pad.at[m % 2], prior(block, tx_ref, block), rows, kx_ref[:, here]).astype(F32)
        stepped = x_conv * step_wide
        x_step[m % 2] = stepped.astype(BF16)
        lines = cum_t[block]
        middle = cum_wide[half - 1 : half]
        scaled = (stepped[:half] * jnp.exp2(middle - cum_wide[:half])).astype(BF16)
        late = jnp.dot(cross[...], scaled, preferred_element_type=F32)
        late = late * jnp.exp2(cum_wide[half:] - middle)
        gate = silu_of_twice(gate_ref[:, here].astype(F32) * 0.5)
        g_ref[:, here] = (jnp.exp2(cum_wide) * gate).astype(BF16)
        for a in range(2):
            at = slice(a * half, (a + 1) * half)
            parts = []
            for j in range(HB):
                column = cum_wide[at, j * HEAD_DIM : j * HEAD_DIM + 1]
                line = lines[j : j + 1, at]
                weights = scores[at, :] * jnp.exp2(jnp.minimum(column - line, 0.0))
                parts.append(
                    jnp.dot(
                        weights.astype(BF16),
                        x_step[m % 2, at, j * HEAD_DIM : (j + 1) * HEAD_DIM],
                        preferred_element_type=F32,
                    )
                )
            inside = jnp.concatenate(parts, axis=1)
            if a == 1:
                inside = inside + late
            a_ref[at, here] = (inside * gate[at]).astype(BF16)


def within_block(core, x, gate, b, c, step, halo, x_recv, b_recv, c_recv, kernel_x, kernel_b, kernel_c, bias, fading):
    heads = step.shape[1]
    width = 4 * WIDE
    steps = x.shape[1] // width
    per_group = steps // (b.shape[1] // STATE)
    full = lambda k, s: (0, 0)
    group = lambda k, s: (0, k // per_group)
    one = lambda k, s: (0, k)
    return pl.pallas_call(
        within_kernel,
        grid_spec=pltpu.PrefetchScalarGridSpec(
            num_scalar_prefetch=1,
            grid=(steps,),
            in_specs=[
                pl.BlockSpec((BLOCK, width), one),
                pl.BlockSpec((BLOCK, width), one),
                pl.BlockSpec((BLOCK, STATE), group),
                pl.BlockSpec((BLOCK, STATE), group),
                pl.BlockSpec((BLOCK, heads), full),
                IN_VMEM,
                IN_VMEM,
                IN_VMEM,
                IN_VMEM,
                pl.BlockSpec((4, width), one),
                pl.BlockSpec((4, STATE), group),
                pl.BlockSpec((4, STATE), group),
                pl.BlockSpec((1, heads), full),
                pl.BlockSpec((1, heads), full),
            ],
            out_specs=[
                pl.BlockSpec((BLOCK, width), one),
                pl.BlockSpec((BLOCK, width), one),
                pl.BlockSpec((BLOCK, STATE), group),
            ],
            scratch_shapes=[
                pltpu.VMEM((2, BLOCK + 8, WIDE), F32),
                pltpu.VMEM((2, BLOCK, 3 * heads), BF16),
                pltpu.VMEM((heads // HB, 8, BLOCK), F32),
                pltpu.VMEM((BLOCK, BLOCK // 2), F32),
                pltpu.VMEM((BLOCK // 2, BLOCK // 2), BF16),
                pltpu.VMEM((2, BLOCK, WIDE), BF16),
            ],
        ),
        out_shape=[
            jax.ShapeDtypeStruct(x.shape, BF16),
            jax.ShapeDtypeStruct(x.shape, BF16),
            jax.ShapeDtypeStruct(c.shape, BF16),
        ],
        compiler_params=pltpu.CompilerParams(vmem_limit_bytes=VMEM),
        cost_estimate=pl.CostEstimate(flops=8_000_000_000, bytes_accessed=12_000_000, transcendentals=6_000_000),
        name="within_block",
    )(
        core, hbm(x), hbm(gate), hbm(b), hbm(c), hbm(step), vmem(halo), vmem(x_recv), vmem(b_recv),
        vmem(c_recv), hbm(kernel_x), hbm(kernel_b), hbm(kernel_c), hbm(bias), hbm(fading),
    )


def scan_kernel(gathered_ref, _, starts_ref, final_ref, decays, inputs, b_rows):
    chips, part, _ = starts_ref.shape
    r = pl.program_id(0)

    @pl.when(r == 0)
    def _():
        extra = [gathered_ref[n, STATE : STATE + 16, :].astype(F32) for n in range(chips)]
        packed = jnp.concatenate([value[0:1] for value in extra], axis=0).astype(BF16)
        row = lax.broadcasted_iota(jnp.int32, (WIDE, WIDE), 0)
        col = lax.broadcasted_iota(jnp.int32, (WIDE, WIDE), 1)
        wide = [
            jnp.dot(packed, (row == col // HEAD_DIM * HEAD_DIM + 8 * q).astype(BF16), preferred_element_type=F32)
            for q in range(6)
        ]
        decays[...] = wide[0] + wide[1] + wide[2]
        pad = jnp.zeros((13, WIDE), F32)
        for n in range(chips):
            x_sums, b_sums = extra[n][1:4], extra[n][7:10]
            if n:
                x_sums = x_sums + extra[n - 1][4:7]
                b_sums = b_sums + extra[n - 1][10:13]
            x_conv = silu_of_twice(x_sums).astype(BF16).astype(F32)
            weight = jnp.concatenate([wide[3 + t][n : n + 1] for t in range(3)], axis=0)
            inputs[n] = jnp.concatenate([x_conv * weight, pad], axis=0).astype(BF16)
            b_rows[n] = jnp.concatenate([silu_of_twice(b_sums), pad], axis=0).astype(BF16)

    rows = pl.ds(pl.multiple_of(r * part, part), part)
    state = jnp.zeros((part, WIDE), F32)
    for n in range(chips):
        starts_ref[n] = state.astype(BF16)
        term = lax.dot_general(
            b_rows[n, :, rows], inputs[n], (((0,), (0,)), ((), ())), preferred_element_type=F32
        )
        state = state * decays[n : n + 1, :] + (gathered_ref[n, rows, :].astype(F32) + term)
    final_ref[rows, :] = state


def scan_states(gathered, after):
    chips = gathered.shape[0]
    part = STATE // 2
    return pl.pallas_call(
        scan_kernel,
        grid=(2,),
        in_specs=[IN_VMEM, IN_HBM],
        out_specs=[pl.BlockSpec((chips, part, WIDE), lambda r: (0, r, 0)), IN_VMEM],
        out_shape=[
            pltpu.HBM((chips, STATE, WIDE), BF16),
            pltpu.VMEM((STATE, WIDE), F32),
        ],
        scratch_shapes=[
            pltpu.VMEM((chips, WIDE), F32),
            pltpu.VMEM((chips, 16, WIDE), BF16),
            pltpu.VMEM((chips, 16, STATE), BF16),
        ],
        compiler_params=pltpu.CompilerParams(vmem_limit_bytes=SMALL),
        cost_estimate=pl.CostEstimate(flops=20_000_000, bytes_accessed=2_500_000, transcendentals=0),
        name="scan_states",
    )(vmem(gathered), hbm(after))


def start_kernel(core_ref, start_ref, first_ref, decay_ref, _, keep_ref, send_ref):
    even = core_ref[0] == 0
    for j in range(first_ref.shape[0]):
        n = pl.program_id(0) * first_ref.shape[0] + j
        start = start_ref[n].astype(F32)
        later = start * decay_ref[j, 0:1, :] + first_ref[j].astype(F32)
        keep_ref[n] = jnp.where(even, start, later).astype(BF16)
        send_ref[n] = jnp.where(even, later, start).astype(BF16)


def block_starts(core, chip_start, first_update, first_decay, after):
    shape = pltpu.VMEM(chip_start.shape, BF16)
    return pl.pallas_call(
        start_kernel,
        grid=(chip_start.shape[0] // 2,),
        in_specs=[
            pl.BlockSpec(memory_space=pltpu.SMEM),
            IN_VMEM,
            pl.BlockSpec((2, STATE, WIDE), lambda i: (i, 0, 0)),
            pl.BlockSpec((2, 8, WIDE), lambda i: (i, 0, 0)),
            IN_HBM,
        ],
        out_specs=[IN_VMEM, IN_VMEM],
        out_shape=[shape, shape],
        compiler_params=pltpu.CompilerParams(vmem_limit_bytes=SMALL),
        cost_estimate=pl.CostEstimate(flops=2_000_000, bytes_accessed=4_500_000, transcendentals=0),
        name="block_starts",
    )(core, vmem(chip_start), hbm(first_update), hbm(first_decay), hbm(after))


def finish_kernel(core_ref, a_ref, g_ref, cc_ref, keep_ref, recv_ref, gain_ref, out_ref, y_ref):
    core = core_ref[0]
    rows, width = out_ref.shape
    n, r = pl.program_id(0), pl.program_id(1)
    at_rows = pl.ds(pl.multiple_of(r * rows, rows), rows)
    per_group = keep_ref.shape[0] // pl.num_programs(0)
    total = jnp.zeros((rows, 1), F32)
    c_conv = cc_ref[at_rows, pl.ds(pl.multiple_of(n * STATE, STATE), STATE)]
    for j in range(per_group):
        for state_ref, parity in ((keep_ref, core), (recv_ref, 1 - core)):
            block = 2 * j + parity
            at = pl.ds(pl.multiple_of(n * width + block * WIDE, WIDE), WIDE)
            carried = jnp.dot(c_conv, state_ref[n * per_group + j], preferred_element_type=F32)
            y = a_ref[at_rows, at].astype(F32) + carried * g_ref[at_rows, at].astype(F32)
            y_ref[:, pl.ds(pl.multiple_of(block * WIDE, WIDE), WIDE)] = y
            total = total + jnp.sum(y * y, axis=1, keepdims=True)
    inverse = 1.0 / jnp.sqrt(total / width + epsilon)
    out_ref[...] = (y_ref[...] * inverse * gain_ref[...]).astype(BF16)


def finish(core, a, g, cc, keep, recv, gain):
    tokens, channels = a.shape
    groups = cc.shape[1] // STATE
    width = channels // groups
    rows = tokens // 2
    return pl.pallas_call(
        finish_kernel,
        grid=(groups, 2),
        in_specs=[
            pl.BlockSpec(memory_space=pltpu.SMEM),
            IN_VMEM,
            IN_VMEM,
            IN_VMEM,
            IN_VMEM,
            IN_VMEM,
            pl.BlockSpec((1, width), lambda n, r: (0, n)),
        ],
        out_specs=pl.BlockSpec((rows, width), lambda n, r: (r, n)),
        scratch_shapes=[pltpu.VMEM((rows, width), F32)],
        out_shape=jax.ShapeDtypeStruct((tokens, channels), BF16),
        compiler_params=pltpu.CompilerParams(vmem_limit_bytes=SMALL),
        cost_estimate=pl.CostEstimate(flops=600_000_000, bytes_accessed=9_000_000, transcendentals=1000),
        name="finish",
    )(core, vmem(a), vmem(g), vmem(cc), vmem(keep), vmem(recv), gain)


def slots_kernel(owners_ref, rank_ref, state_ref, o0, o1, o2, o3):
    outs = (o0, o1, o2, o3)
    for out in outs:
        out[...] = jnp.zeros(out.shape, F32)
    for j in range(HB):
        owner = owners_ref[j]
        slot = jnp.int32(0)
        for i in range(j):
            slot = slot + (owners_ref[i] == owner).astype(jnp.int32)
        piece = state_ref[:, j * HEAD_DIM : (j + 1) * HEAD_DIM].T
        for d, out in enumerate(outs):
            for r in range(out.shape[0]):

                @pl.when((owner == rank_ref[0] ^ d) & (slot == r))
                def _(out=out, r=r, piece=piece):
                    out[r] = piece


def final_slots(owners, rank, state, dests, capacity):
    one = pltpu.VMEM((capacity, HEAD_DIM, STATE), F32)
    smem = pl.BlockSpec(memory_space=pltpu.SMEM)
    return pl.pallas_call(
        slots_kernel,
        in_specs=[smem, smem, IN_VMEM],
        out_specs=[IN_VMEM] * dests,
        out_shape=[one] * dests,
        compiler_params=pltpu.CompilerParams(vmem_limit_bytes=SMALL),
        name="final_slots",
    )(owners, rank, vmem(state))


def local(
    x_input, b_input, output_projection_input, step_input, gate_input, kernel_x, kernel_b, kernel_c,
    step_bias, fading_logarithm, norm_gain, owner_map,
):
    ctx_count = lax.axis_size("ctx")
    ctx_rank = lax.axis_index("ctx")
    dec_count = lax.axis_size("dec")
    dec_rank = lax.axis_index("dec")
    core = ctx_rank % 2
    core_arg = core.astype(jnp.int32).reshape(1)
    x = x_input[0]
    b = b_input[0]
    c = output_projection_input[0]
    step = step_input[0]
    bias = step_bias.reshape(1, -1)
    fading = fading_logarithm.reshape(1, -1)

    swap = [(i, i ^ 1) for i in range(ctx_count)]
    x_recv, b_recv, step_recv = (
        lax.ppermute(x, "ctx", swap),
        lax.ppermute(b, "ctx", swap),
        lax.ppermute(step, "ctx", swap),
    )
    *own, tail = own_updates(core_arg, x, b, c, step, kernel_x, kernel_b, bias, fading)
    tail, step_recv = lax.optimization_barrier((tail, step_recv))
    from_even = lax.ppermute(tail, "ctx", [(i, i + 1) for i in range(1, ctx_count - 1, 2)])
    updates, first_update, first_decay, edge = chip_updates(
        core_arg, own, x, b, x_recv, b_recv, step_recv, kernel_x, kernel_b, bias, fading
    )
    c_recv = lax.ppermute(c, "ctx", swap)
    from_odd = lax.ppermute(from_even, "ctx", swap)
    updates, from_even = lax.optimization_barrier((updates, from_even))
    same_core = [[2 * i + j for i in range(ctx_count // 2)] for j in range(2)]
    gathered = lax.all_to_all(updates, "ctx", 0, 0, axis_index_groups=same_core, tiled=True)
    a, g, cc = within_block(
        core_arg, x, gate_input[0], b, c, step, from_even, x_recv, b_recv, c_recv,
        kernel_x, kernel_b, kernel_c, bias, fading,
    )
    first_update = whole_first(core_arg, first_update, edge, from_even, from_odd, kernel_x, kernel_b)
    starts, state = scan_states(gathered, cc)
    chip_start = lax.all_to_all(starts, "ctx", 0, 0, axis_index_groups=same_core, tiled=True)

    owners = lax.dynamic_slice_in_dim(owner_map[0, :, 0], ctx_rank * HB, HB)
    outgoing = final_slots(owners, dec_rank.astype(jnp.int32).reshape(1), state, dec_count, 2)
    arrived = jnp.zeros((dec_count,) + outgoing[0].shape, F32)
    for d in range(dec_count):
        piece = outgoing[d]
        if d:
            piece = lax.ppermute(piece, "dec", [(i, i ^ d) for i in range(dec_count)])
        arrived = lax.dynamic_update_index_in_dim(arrived, piece, dec_rank ^ d, 0)

    keep, send = block_starts(core_arg, chip_start, first_update, first_decay, arrived)
    recv = lax.ppermute(send, "ctx", swap)
    mixer_rows = finish(core_arg, a, g, cc, keep, recv, norm_gain.reshape(1, -1))
    return (mixer_rows[None], arrived[None, :, None])


def solution(mesh):
    return jax.shard_map(
        local,
        mesh=mesh,
        in_specs=(
            P("dec", "ctx", "tp"),
            P("dec", "ctx", "tp"),
            P("dec", "ctx", "tp"),
            P("dec", "ctx", "tp"),
            P("dec", "ctx", "tp"),
            P(None, "tp"),
            P(None, "tp"),
            P(None, "tp"),
            P("tp"),
            P("tp"),
            P("tp"),
            P("dec", "tp", None),
        ),
        out_specs=(P("dec", "ctx", "tp"), P("dec", None, ("tp", "ctx"), None, None, None)),
        check_vma=False,
    )
```

```python
import functools

import jax
import jax.numpy as jnp
from jax import lax
from jax.experimental import pallas as pl
from jax.experimental.pallas import tpu as pltpu
from jax.sharding import PartitionSpec as P

HEAD_DIM = 64
STATE = 256
BLOCK = 256
HB = 4
WIDE = HB * HEAD_DIM
LOG2E = 1.4426950408889634
VMEM = 40 * 1024 * 1024
SMALL = 12 * 1024 * 1024
IN_VMEM = pl.BlockSpec(memory_space=pltpu.VMEM)
IN_HBM = pl.BlockSpec(memory_space=pl.ANY)


def hbm(value):
    return pltpu.with_memory_space_constraint(value, pltpu.HBM)


def vmem(value):
    return pltpu.with_memory_space_constraint(value, pltpu.VMEM)

epsilon = 1e-05
F32 = jnp.float32
BF16 = jnp.bfloat16
HIGHEST = lax.Precision.HIGHEST


def split3(value):
    high = value.astype(BF16)
    rest = value - high.astype(F32)
    middle = rest.astype(BF16)
    low = (rest - middle.astype(F32)).astype(BF16)
    return high, middle, low


def softplus(value):
    return jnp.maximum(value, 0.0) + jnp.log1p(jnp.exp(-jnp.abs(value)))


def silu_of_twice(half):
    return half + half * jnp.tanh(half)


def spread(rows, width, first_head, heads):
    row = lax.broadcasted_iota(jnp.int32, (rows, width), 0)
    channel = lax.broadcasted_iota(jnp.int32, (rows, width), 1)
    head = row % heads
    return (head == first_head + channel // HEAD_DIM).astype(BF16)


def conv(pad_ref, prior, rows, taps):
    count = rows.shape[0]
    pad_ref[0:8, :] = prior
    pad_ref[8 : 8 + count, :] = rows
    taps = taps.astype(F32) * 0.5
    running = taps[0:1] * pad_ref[5 : 5 + count, :]
    for j in range(1, 4):
        running = running + taps[j : j + 1] * pad_ref[5 + j : 5 + j + count, :]
    return silu_of_twice(running).astype(BF16)


def edge_sums(prior, rows, taps):
    both = jnp.concatenate([prior, rows], axis=0)
    taps = taps.astype(F32) * 0.5
    running = taps[0:1] * both[5:13]
    for j in range(1, 4):
        running = running + taps[j : j + 1] * both[5 + j : 13 + j]
    return running


def steps_of(step, bias, fading):
    step = step.astype(F32).T
    size = softplus(step + bias)
    decay = -size * jnp.exp(fading)
    count = step.shape[0]
    row = lax.broadcasted_iota(jnp.int32, (count, count), 0)
    col = lax.broadcasted_iota(jnp.int32, (count, count), 1)
    lower = (row >= col).astype(BF16)
    pieces = jnp.concatenate(split3(decay), axis=1)
    sums = jnp.dot(lower, pieces, preferred_element_type=F32)
    heads = step.shape[1]
    cumulative = sums[:, :heads] + sums[:, heads : 2 * heads] + sums[:, 2 * heads :]
    return size, cumulative


def lanes(block, width=WIDE):
    return pl.ds(pl.multiple_of(block * width, width), width)


def weights_of(step, bias, fading):
    size, cumulative = steps_of(step, bias, fading)
    last = cumulative[-1:]
    high, middle, _ = split3(size * jnp.exp(last - cumulative))
    return jnp.concatenate([high, middle], axis=1), last


def whole(value):
    return pl.BlockSpec(value.shape, lambda *_: (0,) * value.ndim)


def own_kernel(
    core_ref, x_ref, b_ref, ct_ref, step_ref, kx_ref, kb_ref, bias_ref, fading_ref,
    u_ref, first_weight_ref, closing_ref, tail_ref, pad, weight,
):
    n = pl.program_id(0)
    core = core_ref[0]
    heads = step_ref.shape[0]
    per_group = u_ref.shape[0] // 2
    end = slice(BLOCK - 16, BLOCK)
    x_width, b_width = x_ref.shape[1], b_ref.shape[1]
    tail_ref[:, lanes(n, x_width)] = x_ref[end, :]
    tail_ref[:, lanes(2 * x_width // b_width + n, b_width)] = b_ref[end, :]
    tail_ref[:, 2 * (x_width + b_width) :] = ct_ref[...]

    @pl.when(n == 0)
    def _():
        value, last = weights_of(step_ref[...], bias_ref[...], fading_ref[...])
        first_weight_ref[...] = value[0:16]
        closing_ref[...] = jnp.broadcast_to(last, (8, heads))
        row = lax.broadcasted_iota(jnp.int32, value.shape, 0)
        weight[...] = jnp.where(row < 8, 0.0, value.astype(F32)).astype(BF16)

    none = jnp.zeros((8, STATE), F32)
    b_t = conv(pad.at[0], none, b_ref[...].astype(F32), kb_ref[...]).astype(F32).T.astype(BF16)
    for j in range(per_group):
        block = 2 * j + core
        at = lanes(block)
        x_conv = conv(pad.at[j % 2], none, x_ref[:, at].astype(F32), kx_ref[:, at]).astype(F32)
        select = spread(2 * heads, WIDE, (2 * per_group * n + block) * HB, heads)
        inputs = x_conv * jnp.dot(weight[...], select, preferred_element_type=F32)
        u_ref[n * per_group + j] = jnp.dot(b_t, inputs.astype(BF16), preferred_element_type=F32)


def own_updates(core, x, b, c, step, kernel_x, kernel_b, bias, fading):
    heads = step.shape[0]
    groups = b.shape[1] // STATE
    width = x.shape[1] // groups
    blocks = x.shape[1] // WIDE // 2
    one = lambda n, c: (0, n)
    return pl.pallas_call(
        own_kernel,
        grid_spec=pltpu.PrefetchScalarGridSpec(
            num_scalar_prefetch=1,
            grid=(groups,),
            in_specs=[
                pl.BlockSpec((BLOCK, width), one),
                pl.BlockSpec((BLOCK, STATE), one),
                pl.BlockSpec((16, c.shape[1]), lambda n, s: (BLOCK // 16 - 1, 0)),
                whole(step),
                pl.BlockSpec((4, width), one),
                pl.BlockSpec((4, STATE), one),
                whole(bias),
                whole(fading),
            ],
            out_specs=[IN_VMEM, IN_VMEM, IN_VMEM, IN_VMEM],
            scratch_shapes=[
                pltpu.VMEM((2, BLOCK + 8, WIDE), F32),
                pltpu.VMEM((BLOCK, 2 * heads), BF16),
            ],
        ),
        out_shape=[
            pltpu.VMEM((blocks, STATE, WIDE), F32),
            pltpu.VMEM((16, 2 * heads), BF16),
            pltpu.VMEM((8, heads), F32),
            pltpu.VMEM((16, x.shape[1] + b.shape[1] + c.shape[1]), BF16),
        ],
        compiler_params=pltpu.CompilerParams(vmem_limit_bytes=VMEM),
        cost_estimate=pl.CostEstimate(flops=300_000_000, bytes_accessed=10_000_000, transcendentals=600_000),
        name="own_updates",
    )(core, hbm(x), hbm(b), hbm(c), hbm(step), hbm(kernel_x), hbm(kernel_b), hbm(bias), hbm(fading))


def chip_kernel(
    core_ref, u_own_ref, first_weight_ref, closing_ref, xh_ref, xt_ref, bh_ref, bt_ref, xr_ref, br_ref,
    sr_ref, kx_ref, kb_ref, bias_ref, fading_ref,
    u_ref, first_ref, decay_ref, edge_ref, pad, small, extra, weight, weight_first, values,
):
    n = pl.program_id(0)
    core = core_ref[0]
    even = core == 0
    heads = sr_ref.shape[0]
    per_group = u_ref.shape[0]
    head8 = slice(0, 8)
    tail8 = slice(8, 16)

    @pl.when(n == 0)
    def _():
        value, last = weights_of(sr_ref[...], bias_ref[...], fading_ref[...])
        row = lax.broadcasted_iota(jnp.int32, value.shape, 0)
        weight[...] = jnp.where((row < 3) & jnp.logical_not(even), 0.0, value.astype(F32)).astype(BF16)
        mine = first_weight_ref[...].astype(F32)
        row = lax.broadcasted_iota(jnp.int32, mine.shape, 0)
        dropped = (row >= 8) | ((row < 3) & even)
        weight_first[...] = jnp.where(dropped, 0.0, mine).astype(BF16)
        edge = jnp.where(even, mine, value[0:16].astype(F32))
        edge = edge[:, :heads] + edge[:, heads:]
        own = jnp.exp(closing_ref[0:1, :])
        other = jnp.exp(last)
        values[0:1, :] = own
        values[1:2, :] = other
        values[2:3, :] = jnp.exp(closing_ref[0:1, :] + last)
        values[3:6, :] = edge[0:3] * jnp.where(even, other, own)
        values[6:9, :] = edge[0:3]
        values[9:16, :] = jnp.zeros((7, heads), F32)

    def edges(own_head, own_end, recv_head, recv_end, taps):
        none = jnp.zeros(own_head.shape, F32)
        first = edge_sums(none, jnp.where(even, own_head, recv_head), taps)
        last = edge_sums(jnp.where(even, recv_end, own_end), none, taps)
        return jnp.where(even, none, recv_end), jnp.where(even, own_end, none), first, last

    def rows_of(ref, rows, at):
        return ref[rows, at].astype(F32)

    end = slice(BLOCK - 16, BLOCK)
    at = lanes(n, STATE)
    everything = slice(None)
    prior_own, prior_recv, b_first, b_last = edges(
        rows_of(bh_ref, slice(0, 16), everything)[head8],
        rows_of(bt_ref, slice(0, 16), everything)[tail8],
        rows_of(br_ref, slice(0, 16), at)[head8],
        rows_of(br_ref, end, at)[tail8],
        kb_ref[...],
    )
    b_own = conv(small.at[0], prior_own, bh_ref[...].astype(F32), kb_ref[...])
    b_recv = conv(pad.at[0], prior_recv, br_ref[:, at].astype(F32), kb_ref[...])
    b_own = b_own.astype(F32).T.astype(BF16)
    b_recv = b_recv.astype(F32).T.astype(BF16)
    pieces = jnp.concatenate(split3(values[...]), axis=1)
    for j in range(per_group):
        block = 2 * j + core
        head = (2 * per_group * n + block) * HB
        here = lanes(block)
        at = lanes(2 * per_group * n + block)
        taps = kx_ref[:, here]
        select = spread(2 * heads, WIDE, head, heads)
        prior_own, prior_recv, x_first, x_last = edges(
            rows_of(xh_ref, slice(0, 16), here)[head8],
            rows_of(xt_ref, slice(0, 16), here)[tail8],
            rows_of(xr_ref, slice(0, 16), at)[head8],
            rows_of(xr_ref, end, at)[tail8],
            taps,
        )
        x_own = conv(small.at[j % 2], prior_own, xh_ref[:, here].astype(F32), taps).astype(F32)
        x_own = x_own * jnp.dot(weight_first[...], select, preferred_element_type=F32)
        x_conv = conv(pad.at[j % 2], prior_recv, xr_ref[:, at].astype(F32), taps).astype(F32)
        inputs = x_conv * jnp.dot(weight[...], select, preferred_element_type=F32)
        u_recv = jnp.dot(b_recv, inputs.astype(BF16), preferred_element_type=F32)
        u_own = u_own_ref[n * per_group + j] + jnp.dot(
            b_own, x_own.astype(BF16), preferred_element_type=F32
        )
        wide = jnp.dot(pieces, spread(3 * heads, WIDE, head, heads), preferred_element_type=F32)
        own_factor = jnp.where(even, wide[1:2], 1.0)
        recv_factor = jnp.where(even, 1.0, wide[0:1])
        u_ref[j, 0:STATE, :] = (u_own * own_factor + u_recv * recv_factor).astype(BF16)
        first_ref[j] = jnp.where(even, u_own, u_recv).astype(BF16)
        decay_ref[j] = jnp.broadcast_to(jnp.where(even, wide[0:1], wide[1:2]), (8, WIDE))
        high, middle, low = split3(wide[2:3])
        place = lax.broadcasted_iota(jnp.int32, (1, WIDE), 1) % HEAD_DIM // 8
        packed = jnp.zeros((1, WIDE), F32)
        for q, value in enumerate((high, middle, low, wide[3:4], wide[4:5], wide[5:6])):
            packed = jnp.where(place == q, value.astype(F32), packed)
        extra[0:1, :] = packed
        extra[1:4, :] = x_first[0:3]
        extra[4:7, :] = x_last[0:3]
        extra[7:10, :] = b_first[0:3]
        extra[10:13, :] = b_last[0:3]
        extra[13:16, :] = jnp.zeros((3, WIDE), F32)
        u_ref[j, STATE : STATE + 16, :] = extra[...].astype(BF16)
        edge_ref[j, 0:3, :] = x_first[0:3]
        edge_ref[j, 3:6, :] = b_first[0:3]
        edge_ref[j, 6:9, :] = wide[6:9]
        edge_ref[j, 9:16, :] = jnp.zeros((7, WIDE), F32)


def chip_updates(core, own, x, b, x_recv, b_recv, step_recv, kernel_x, kernel_b, bias, fading):
    u_own, first_weight, closing = own
    heads = step_recv.shape[0]
    groups = b.shape[1] // STATE
    width = x.shape[1] // groups
    blocks = x.shape[1] // WIDE // 2
    per_group = blocks // groups
    end = BLOCK // 16 - 1
    one = lambda n, c: (0, n)
    tail = lambda n, c: (end, n)
    out = lambda n, c: (n, 0, 0)
    return pl.pallas_call(
        chip_kernel,
        grid_spec=pltpu.PrefetchScalarGridSpec(
            num_scalar_prefetch=1,
            grid=(groups,),
            in_specs=[
                IN_VMEM,
                IN_VMEM,
                IN_VMEM,
                pl.BlockSpec((16, width), one),
                pl.BlockSpec((16, width), tail),
                pl.BlockSpec((16, STATE), one),
                pl.BlockSpec((16, STATE), tail),
                IN_VMEM,
                IN_VMEM,
                IN_VMEM,
                pl.BlockSpec((4, width), one),
                pl.BlockSpec((4, STATE), one),
                whole(bias),
                whole(fading),
            ],
            out_specs=[
                pl.BlockSpec((per_group, STATE + 16, WIDE), out),
                pl.BlockSpec((per_group, STATE, WIDE), out),
                pl.BlockSpec((per_group, 8, WIDE), out),
                pl.BlockSpec((per_group, 16, WIDE), out),
            ],
            scratch_shapes=[
                pltpu.VMEM((2, BLOCK + 8, WIDE), F32),
                pltpu.VMEM((2, 24, WIDE), F32),
                pltpu.VMEM((16, WIDE), F32),
                pltpu.VMEM((BLOCK, 2 * heads), BF16),
                pltpu.VMEM((16, 2 * heads), BF16),
                pltpu.VMEM((16, heads), F32),
            ],
        ),
        out_shape=[
            pltpu.HBM((blocks, STATE + 16, WIDE), BF16),
            pltpu.HBM((blocks, STATE, WIDE), BF16),
            pltpu.HBM((blocks, 8, WIDE), F32),
            pltpu.HBM((blocks, 16, WIDE), F32),
        ],
        compiler_params=pltpu.CompilerParams(vmem_limit_bytes=VMEM),
        cost_estimate=pl.CostEstimate(flops=300_000_000, bytes_accessed=10_000_000, transcendentals=600_000),
        name="chip_updates",
    )(
        core, vmem(u_own), vmem(first_weight), vmem(closing), hbm(x), hbm(x), hbm(b), hbm(b), vmem(x_recv),
        vmem(b_recv), vmem(step_recv), hbm(kernel_x), hbm(kernel_b), hbm(bias), hbm(fading),
    )


def edge_kernel(core_ref, first_ref, edge_ref, he_ref, ho_ref, kx_ref, kb_ref, out_ref):
    n = pl.program_id(0)
    core = core_ref[0]
    even = core == 0
    per_group = first_ref.shape[0]
    blocks = 2 * per_group * pl.num_programs(0)
    none = jnp.zeros((8, WIDE), F32)
    row = lax.broadcasted_iota(jnp.int32, (16, WIDE), 0)

    def from_halo(at, taps):
        halo = jnp.where(even, he_ref[:, at].astype(F32), ho_ref[:, at].astype(F32))[8:]
        return edge_sums(halo, none, taps)[0:3]

    b_sums = from_halo(lanes(blocks + n, STATE), kb_ref[...])
    for j in range(per_group):
        block = 2 * j + core
        x_sums = from_halo(lanes(2 * per_group * n + block), kx_ref[:, lanes(block)])
        rows = edge_ref[j]
        x_conv = silu_of_twice(rows[0:3] + x_sums).astype(BF16).astype(F32)
        b_conv = silu_of_twice(rows[3:6] + b_sums)
        inputs = x_conv * rows[6:9]
        pad = jnp.zeros((13, WIDE), F32)
        inputs = jnp.concatenate([inputs, pad], axis=0).astype(BF16)
        b_conv = jnp.concatenate([b_conv, pad], axis=0).astype(BF16)
        term = lax.dot_general(b_conv, inputs, (((0,), (0,)), ((), ())), preferred_element_type=F32)
        out_ref[j] = (first_ref[j].astype(F32) + term).astype(BF16)


def whole_first(core, first, edge, halo_even, halo_odd, kernel_x, kernel_b):
    groups = kernel_b.shape[1] // STATE
    per_group = first.shape[0] // groups
    width = kernel_x.shape[1] // groups
    out = lambda n, c: (n, 0, 0)
    one = lambda n, c: (0, n)
    return pl.pallas_call(
        edge_kernel,
        grid_spec=pltpu.PrefetchScalarGridSpec(
            num_scalar_prefetch=1,
            grid=(groups,),
            in_specs=[
                pl.BlockSpec((per_group, STATE, WIDE), out),
                pl.BlockSpec((per_group, 16, WIDE), out),
                IN_VMEM,
                IN_VMEM,
                pl.BlockSpec((4, width), one),
                pl.BlockSpec((4, STATE), one),
            ],
            out_specs=pl.BlockSpec((per_group, STATE, WIDE), out),
        ),
        out_shape=pltpu.HBM(first.shape, BF16),
        compiler_params=pltpu.CompilerParams(vmem_limit_bytes=SMALL),
        cost_estimate=pl.CostEstimate(flops=30_000_000, bytes_accessed=3_000_000, transcendentals=10_000),
        name="whole_first",
    )(core, hbm(first), hbm(edge), vmem(halo_even), vmem(halo_odd), hbm(kernel_x), hbm(kernel_b))


def within_kernel(
    core_ref, x_ref, gate_ref, b_ref, c_ref, step_ref, halo_ref, tx_ref, tb_ref, tc_ref,
    kx_ref, kb_ref, kc_ref, bias_ref, fading_ref, a_ref, g_ref, cc_ref, pad, pieces, cum_t, scores, cross, x_step,
):
    k = pl.program_id(0)
    even = core_ref[0] == 0
    heads = step_ref.shape[0]
    half = BLOCK // 2
    steps = pl.num_programs(0)
    blocks = x_ref.shape[1] // WIDE
    group = k // (steps // 2)
    end = slice(BLOCK - 16, BLOCK)

    def prior(halo_at, tail_ref, at):
        halo = halo_ref[:, lanes(halo_at)].astype(F32)
        return jnp.where(even, halo, tail_ref[end, lanes(at)].astype(F32))[8:]

    @pl.when(k == 0)
    def _():
        size, cumulative = steps_of(step_ref[...], bias_ref[...], fading_ref[...])
        cumulative = cumulative * LOG2E
        pieces[0] = jnp.concatenate(split3(cumulative), axis=1)
        pieces[1] = jnp.concatenate(split3(size), axis=1)
        turned = cumulative.T
        for n in range(heads // HB):
            cum_t[n, 0:HB, :] = turned[n * HB : (n + 1) * HB]

    @pl.when(k % (steps // 2) == 0)
    def _():
        in_halo = steps * blocks + group
        b_conv = conv(pad.at[0], prior(in_halo, tb_ref, group), b_ref[...].astype(F32), kb_ref[...])
        c_conv = conv(pad.at[1], prior(in_halo + 2, tc_ref, group), c_ref[...].astype(F32), kc_ref[...])
        cc_ref[...] = c_conv
        products = lax.dot_general(
            c_conv, b_conv, (((1,), (1,)), ((), ())), preferred_element_type=F32
        )
        row = lax.broadcasted_iota(jnp.int32, (half, half), 0)
        col = lax.broadcasted_iota(jnp.int32, (half, half), 1)
        for a in range(2):
            at = slice(a * half, (a + 1) * half)
            scores[at, :] = jnp.where(row >= col, products[at, at], 0.0)
        cross[...] = products[half:, :half].astype(BF16)

    for m in range(blocks):
        block = k * blocks + m
        here = slice(m * WIDE, (m + 1) * WIDE)
        select = spread(3 * heads, WIDE, block * HB, heads)
        cum_wide = jnp.dot(pieces[0], select, preferred_element_type=F32)
        step_wide = jnp.dot(pieces[1], select, preferred_element_type=F32)
        rows = x_ref[:, here].astype(F32)
        x_conv = conv(pad.at[m % 2], prior(block, tx_ref, block), rows, kx_ref[:, here]).astype(F32)
        stepped = x_conv * step_wide
        x_step[m % 2] = stepped.astype(BF16)
        lines = cum_t[block]
        middle = cum_wide[half - 1 : half]
        scaled = (stepped[:half] * jnp.exp2(middle - cum_wide[:half])).astype(BF16)
        late = jnp.dot(cross[...], scaled, preferred_element_type=F32)
        late = late * jnp.exp2(cum_wide[half:] - middle)
        gate = silu_of_twice(gate_ref[:, here].astype(F32) * 0.5)
        g_ref[:, here] = (jnp.exp2(cum_wide) * gate).astype(BF16)
        for a in range(2):
            at = slice(a * half, (a + 1) * half)
            parts = []
            for j in range(HB):
                column = cum_wide[at, j * HEAD_DIM : j * HEAD_DIM + 1]
                line = lines[j : j + 1, at]
                weights = scores[at, :] * jnp.exp2(jnp.minimum(column - line, 0.0))
                parts.append(
                    jnp.dot(
                        weights.astype(BF16),
                        x_step[m % 2, at, j * HEAD_DIM : (j + 1) * HEAD_DIM],
                        preferred_element_type=F32,
                    )
                )
            inside = jnp.concatenate(parts, axis=1)
            if a == 1:
                inside = inside + late
            a_ref[at, here] = (inside * gate[at]).astype(BF16)


def within_block(core, x, gate, b, c, step, halo, x_recv, b_recv, c_recv, kernel_x, kernel_b, kernel_c, bias, fading):
    heads = step.shape[0]
    width = 4 * WIDE
    steps = x.shape[1] // width
    per_group = steps // (b.shape[1] // STATE)
    full = lambda k, s: (0, 0)
    group = lambda k, s: (0, k // per_group)
    one = lambda k, s: (0, k)
    return pl.pallas_call(
        within_kernel,
        grid_spec=pltpu.PrefetchScalarGridSpec(
            num_scalar_prefetch=1,
            grid=(steps,),
            in_specs=[
                pl.BlockSpec((BLOCK, width), one),
                pl.BlockSpec((BLOCK, width), one),
                pl.BlockSpec((BLOCK, STATE), group),
                pl.BlockSpec((BLOCK, STATE), group),
                whole(step),
                IN_VMEM,
                IN_VMEM,
                IN_VMEM,
                IN_VMEM,
                pl.BlockSpec((4, width), one),
                pl.BlockSpec((4, STATE), group),
                pl.BlockSpec((4, STATE), group),
                pl.BlockSpec((1, heads), full),
                pl.BlockSpec((1, heads), full),
            ],
            out_specs=[
                pl.BlockSpec((BLOCK, width), one),
                pl.BlockSpec((BLOCK, width), one),
                pl.BlockSpec((BLOCK, STATE), group),
            ],
            scratch_shapes=[
                pltpu.VMEM((2, BLOCK + 8, WIDE), F32),
                pltpu.VMEM((2, BLOCK, 3 * heads), BF16),
                pltpu.VMEM((heads // HB, 8, BLOCK), F32),
                pltpu.VMEM((BLOCK, BLOCK // 2), F32),
                pltpu.VMEM((BLOCK // 2, BLOCK // 2), BF16),
                pltpu.VMEM((2, BLOCK, WIDE), BF16),
            ],
        ),
        out_shape=[
            jax.ShapeDtypeStruct(x.shape, BF16),
            jax.ShapeDtypeStruct(x.shape, BF16),
            jax.ShapeDtypeStruct(c.shape, BF16),
        ],
        compiler_params=pltpu.CompilerParams(vmem_limit_bytes=VMEM),
        cost_estimate=pl.CostEstimate(flops=8_000_000_000, bytes_accessed=12_000_000, transcendentals=6_000_000),
        name="within_block",
    )(
        core, hbm(x), hbm(gate), hbm(b), hbm(c), hbm(step), vmem(halo), vmem(x_recv), vmem(b_recv),
        vmem(c_recv), hbm(kernel_x), hbm(kernel_b), hbm(kernel_c), hbm(bias), hbm(fading),
    )


def scan_kernel(gathered_ref, _, starts_ref, final_ref, decays, inputs, b_rows):
    chips, part, _ = starts_ref.shape
    r = pl.program_id(0)

    @pl.when(r == 0)
    def _():
        extra = [gathered_ref[n, STATE : STATE + 16, :].astype(F32) for n in range(chips)]
        packed = jnp.concatenate([value[0:1] for value in extra], axis=0).astype(BF16)
        row = lax.broadcasted_iota(jnp.int32, (WIDE, WIDE), 0)
        col = lax.broadcasted_iota(jnp.int32, (WIDE, WIDE), 1)
        wide = [
            jnp.dot(packed, (row == col // HEAD_DIM * HEAD_DIM + 8 * q).astype(BF16), preferred_element_type=F32)
            for q in range(6)
        ]
        decays[...] = wide[0] + wide[1] + wide[2]
        pad = jnp.zeros((13, WIDE), F32)
        for n in range(chips):
            x_sums, b_sums = extra[n][1:4], extra[n][7:10]
            if n:
                x_sums = x_sums + extra[n - 1][4:7]
                b_sums = b_sums + extra[n - 1][10:13]
            x_conv = silu_of_twice(x_sums).astype(BF16).astype(F32)
            weight = jnp.concatenate([wide[3 + t][n : n + 1] for t in range(3)], axis=0)
            inputs[n] = jnp.concatenate([x_conv * weight, pad], axis=0).astype(BF16)
            b_rows[n] = jnp.concatenate([silu_of_twice(b_sums), pad], axis=0).astype(BF16)

    rows = pl.ds(pl.multiple_of(r * part, part), part)
    state = jnp.zeros((part, WIDE), F32)
    for n in range(chips):
        starts_ref[n] = state.astype(BF16)
        term = lax.dot_general(
            b_rows[n, :, rows], inputs[n], (((0,), (0,)), ((), ())), preferred_element_type=F32
        )
        state = state * decays[n : n + 1, :] + (gathered_ref[n, rows, :].astype(F32) + term)
    final_ref[rows, :] = state


def scan_states(gathered, after):
    chips = gathered.shape[0]
    part = STATE // 2
    return pl.pallas_call(
        scan_kernel,
        grid=(2,),
        in_specs=[IN_VMEM, IN_HBM],
        out_specs=[pl.BlockSpec((chips, part, WIDE), lambda r: (0, r, 0)), IN_VMEM],
        out_shape=[
            pltpu.HBM((chips, STATE, WIDE), BF16),
            pltpu.VMEM((STATE, WIDE), F32),
        ],
        scratch_shapes=[
            pltpu.VMEM((chips, WIDE), F32),
            pltpu.VMEM((chips, 16, WIDE), BF16),
            pltpu.VMEM((chips, 16, STATE), BF16),
        ],
        compiler_params=pltpu.CompilerParams(vmem_limit_bytes=SMALL),
        cost_estimate=pl.CostEstimate(flops=20_000_000, bytes_accessed=2_500_000, transcendentals=0),
        name="scan_states",
    )(vmem(gathered), hbm(after))


def start_kernel(core_ref, start_ref, first_ref, decay_ref, _, keep_ref, send_ref):
    even = core_ref[0] == 0
    for j in range(first_ref.shape[0]):
        n = pl.program_id(0) * first_ref.shape[0] + j
        start = start_ref[n].astype(F32)
        later = start * decay_ref[j, 0:1, :] + first_ref[j].astype(F32)
        keep_ref[n] = jnp.where(even, start, later).astype(BF16)
        send_ref[n] = jnp.where(even, later, start).astype(BF16)


def block_starts(core, chip_start, first_update, first_decay, after):
    shape = pltpu.VMEM(chip_start.shape, BF16)
    return pl.pallas_call(
        start_kernel,
        grid=(chip_start.shape[0] // 4,),
        in_specs=[
            pl.BlockSpec(memory_space=pltpu.SMEM),
            IN_VMEM,
            pl.BlockSpec((4, STATE, WIDE), lambda i: (i, 0, 0)),
            pl.BlockSpec((4, 8, WIDE), lambda i: (i, 0, 0)),
            IN_HBM,
        ],
        out_specs=[IN_VMEM, IN_VMEM],
        out_shape=[shape, shape],
        compiler_params=pltpu.CompilerParams(vmem_limit_bytes=SMALL),
        cost_estimate=pl.CostEstimate(flops=2_000_000, bytes_accessed=4_500_000, transcendentals=0),
        name="block_starts",
    )(core, vmem(chip_start), hbm(first_update), hbm(first_decay), hbm(after))


def carried_rows(n, block, rows, c_conv, state, a_ref, g_ref, width):
    at = pl.ds(pl.multiple_of(n * width + block * WIDE, WIDE), WIDE)
    carried = jnp.dot(c_conv, state, preferred_element_type=F32)
    return a_ref[rows, at].astype(F32) + carried * g_ref[rows, at].astype(F32)


def near_kernel(core_ref, a_ref, g_ref, cc_ref, keep_ref, y_ref, sum_ref):
    n = pl.program_id(0)
    groups = pl.num_programs(0)
    per_group = keep_ref.shape[0] // groups
    width = a_ref.shape[1] // groups
    everything = slice(None)
    c_conv = cc_ref[:, lanes(n, STATE)]
    total = jnp.zeros((BLOCK, 1), F32)
    for j in range(per_group):
        at = n * per_group + j
        block = 2 * j + core_ref[0]
        y = carried_rows(n, block, everything, c_conv, keep_ref[at], a_ref, g_ref, width)
        y_ref[:, lanes(at)] = y
        total = total + jnp.sum(y * y, axis=1, keepdims=True)
    sum_ref[n] = jnp.broadcast_to(total, sum_ref.shape[1:])


def near_rows(core, a, g, cc, keep):
    tokens, channels = a.shape
    groups = cc.shape[1] // STATE
    smem = pl.BlockSpec(memory_space=pltpu.SMEM)
    return pl.pallas_call(
        near_kernel,
        grid=(groups,),
        in_specs=[smem, IN_VMEM, IN_VMEM, IN_VMEM, IN_VMEM],
        out_specs=[IN_VMEM, IN_VMEM],
        out_shape=[pltpu.VMEM((tokens, channels // 2), F32), pltpu.VMEM((groups, tokens, 128), F32)],
        compiler_params=pltpu.CompilerParams(vmem_limit_bytes=SMALL),
        cost_estimate=pl.CostEstimate(flops=300_000_000, bytes_accessed=5_000_000, transcendentals=1000),
        name="near_rows",
    )(core, vmem(a), vmem(g), vmem(cc), vmem(keep))


def finish_kernel(core_ref, a_ref, g_ref, cc_ref, near_ref, sum_ref, recv_ref, gain_ref, out_ref, y_ref):
    core = core_ref[0]
    rows, width = out_ref.shape
    n, r = pl.program_id(0), pl.program_id(1)
    at_rows = pl.ds(pl.multiple_of(r * rows, rows), rows)
    per_group = recv_ref.shape[0] // pl.num_programs(0)
    total = sum_ref[n, at_rows, 0:1]
    c_conv = cc_ref[at_rows, lanes(n, STATE)]
    for j in range(per_group):
        block = 2 * j + 1 - core
        y = carried_rows(n, block, at_rows, c_conv, recv_ref[n * per_group + j], a_ref, g_ref, width)
        y_ref[:, j * WIDE : (j + 1) * WIDE] = y
        total = total + jnp.sum(y * y, axis=1, keepdims=True)
    inverse = 1.0 / jnp.sqrt(total / width + epsilon)
    for j in range(per_group):
        near = near_ref[at_rows, lanes(n * per_group + j)]
        for y, block in ((near, 2 * j + core), (y_ref[:, j * WIDE : (j + 1) * WIDE], 2 * j + 1 - core)):
            out_ref[:, lanes(block)] = (y * inverse * gain_ref[:, lanes(block)]).astype(BF16)


def finish(core, a, g, cc, near, sums, recv, gain):
    tokens, channels = a.shape
    groups = cc.shape[1] // STATE
    width = channels // groups
    rows = tokens
    smem = pl.BlockSpec(memory_space=pltpu.SMEM)
    return pl.pallas_call(
        finish_kernel,
        grid=(groups, 1),
        in_specs=[smem] + [IN_VMEM] * 6 + [pl.BlockSpec((1, width), lambda n, r: (0, n))],
        out_specs=pl.BlockSpec((rows, width), lambda n, r: (r, n)),
        scratch_shapes=[pltpu.VMEM((rows, width // 2), F32)],
        out_shape=jax.ShapeDtypeStruct((tokens, channels), BF16),
        compiler_params=pltpu.CompilerParams(vmem_limit_bytes=SMALL),
        cost_estimate=pl.CostEstimate(flops=300_000_000, bytes_accessed=9_000_000, transcendentals=1000),
        name="finish",
    )(core, vmem(a), vmem(g), vmem(cc), vmem(near), vmem(sums), vmem(recv), gain)


def slots_kernel(owners_ref, rank_ref, state_ref, o0, o1, o2, o3):
    outs = (o0, o1, o2, o3)
    for out in outs:
        out[...] = jnp.zeros(out.shape, F32)
    for j in range(HB):
        owner = owners_ref[j]
        slot = jnp.int32(0)
        for i in range(j):
            slot = slot + (owners_ref[i] == owner).astype(jnp.int32)
        piece = state_ref[:, j * HEAD_DIM : (j + 1) * HEAD_DIM].T
        for d, out in enumerate(outs):
            for r in range(out.shape[0]):

                @pl.when((owner == rank_ref[0] ^ d) & (slot == r))
                def _(out=out, r=r, piece=piece):
                    out[r] = piece


def final_slots(owners, rank, state, dests, capacity):
    one = pltpu.VMEM((capacity, HEAD_DIM, STATE), F32)
    smem = pl.BlockSpec(memory_space=pltpu.SMEM)
    return pl.pallas_call(
        slots_kernel,
        in_specs=[smem, smem, IN_VMEM],
        out_specs=[IN_VMEM] * dests,
        out_shape=[one] * dests,
        compiler_params=pltpu.CompilerParams(vmem_limit_bytes=SMALL),
        name="final_slots",
    )(owners, rank, vmem(state))


def local(
    x_input, b_input, output_projection_input, step_input, gate_input, kernel_x, kernel_b, kernel_c,
    step_bias, fading_logarithm, norm_gain, owner_map,
):
    ctx_count = lax.axis_size("ctx")
    ctx_rank = lax.axis_index("ctx")
    dec_count = lax.axis_size("dec")
    dec_rank = lax.axis_index("dec")
    core = ctx_rank % 2
    core_arg = core.astype(jnp.int32).reshape(1)
    x = x_input[0]
    b = b_input[0]
    c = output_projection_input[0]
    step = step_input[0].T
    bias = step_bias.reshape(1, -1)
    fading = fading_logarithm.reshape(1, -1)

    swap = [(i, i ^ 1) for i in range(ctx_count)]
    x_recv, b_recv, step_recv = (
        lax.ppermute(x, "ctx", swap),
        lax.ppermute(b, "ctx", swap),
        lax.ppermute(step, "ctx", swap),
    )
    *own, tail = own_updates(core_arg, x, b, c, step, kernel_x, kernel_b, bias, fading)
    tail, step_recv = lax.optimization_barrier((tail, step_recv))
    from_even = lax.ppermute(tail, "ctx", [(i, i + 1) for i in range(1, ctx_count - 1, 2)])
    updates, first_update, first_decay, edge = chip_updates(
        core_arg, own, x, b, x_recv, b_recv, step_recv, kernel_x, kernel_b, bias, fading
    )
    c_recv = lax.ppermute(c, "ctx", swap)
    from_odd = lax.ppermute(from_even, "ctx", swap)
    updates, from_even = lax.optimization_barrier((updates, from_even))
    same_core = [[2 * i + j for i in range(ctx_count // 2)] for j in range(2)]
    gathered = lax.all_to_all(updates, "ctx", 0, 0, axis_index_groups=same_core, tiled=True)
    a, g, cc = within_block(
        core_arg, x, gate_input[0], b, c, step, from_even, x_recv, b_recv, c_recv,
        kernel_x, kernel_b, kernel_c, bias, fading,
    )
    first_update = whole_first(core_arg, first_update, edge, from_even, from_odd, kernel_x, kernel_b)
    starts, state = scan_states(gathered, cc)
    chip_start = lax.all_to_all(starts, "ctx", 0, 0, axis_index_groups=same_core, tiled=True)

    owners = lax.dynamic_slice_in_dim(owner_map[0, :, 0], ctx_rank * HB, HB)
    outgoing = final_slots(owners, dec_rank.astype(jnp.int32).reshape(1), state, dec_count, 2)
    arrived = jnp.zeros((dec_count,) + outgoing[0].shape, F32)
    for d in range(dec_count):
        piece = outgoing[d]
        if d:
            piece = lax.ppermute(piece, "dec", [(i, i ^ d) for i in range(dec_count)])
        arrived = lax.dynamic_update_index_in_dim(arrived, piece, dec_rank ^ d, 0)

    keep, send = block_starts(core_arg, chip_start, first_update, first_decay, arrived)
    recv = lax.ppermute(send, "ctx", swap)
    near, sums = near_rows(core_arg, a, g, cc, keep)
    recv, near, sums = lax.optimization_barrier((recv, near, sums))
    mixer_rows = finish(core_arg, a, g, cc, near, sums, recv, norm_gain.reshape(1, -1))
    return (mixer_rows[None], arrived[None, :, None])


def solution(mesh):
    return jax.shard_map(
        local,
        mesh=mesh,
        in_specs=(
            P("dec", "ctx", "tp"),
            P("dec", "ctx", "tp"),
            P("dec", "ctx", "tp"),
            P("dec", "ctx", "tp"),
            P("dec", "ctx", "tp"),
            P(None, "tp"),
            P(None, "tp"),
            P(None, "tp"),
            P("tp"),
            P("tp"),
            P("tp"),
            P("dec", "tp", None),
        ),
        out_specs=(P("dec", "ctx", "tp"), P("dec", None, ("tp", "ctx"), None, None, None)),
        check_vma=False,
    )
```

```python
import functools

import jax
import jax.numpy as jnp
from jax import lax
from jax.experimental import pallas as pl
from jax.experimental.pallas import tpu as pltpu
from jax.sharding import PartitionSpec as P

HEAD_DIM = 64
STATE = 256
BLOCK = 256
HB = 4
WIDE = HB * HEAD_DIM
LOG2E = 1.4426950408889634
VMEM = 40 * 1024 * 1024
SMALL = 12 * 1024 * 1024
IN_VMEM = pl.BlockSpec(memory_space=pltpu.VMEM)
IN_HBM = pl.BlockSpec(memory_space=pl.ANY)


def hbm(value):
    return pltpu.with_memory_space_constraint(value, pltpu.HBM)


def vmem(value):
    return pltpu.with_memory_space_constraint(value, pltpu.VMEM)

epsilon = 1e-05
F32 = jnp.float32
BF16 = jnp.bfloat16
HIGHEST = lax.Precision.HIGHEST


def split3(value):
    high = value.astype(BF16)
    rest = value - high.astype(F32)
    middle = rest.astype(BF16)
    low = (rest - middle.astype(F32)).astype(BF16)
    return high, middle, low


def softplus(value):
    return jnp.maximum(value, 0.0) + jnp.log1p(jnp.exp(-jnp.abs(value)))


def silu_of_twice(half):
    return half + half * jnp.tanh(half)


def spread(rows, width, first_head, heads):
    row = lax.broadcasted_iota(jnp.int32, (rows, width), 0)
    channel = lax.broadcasted_iota(jnp.int32, (rows, width), 1)
    head = row % heads
    return (head == first_head + channel // HEAD_DIM).astype(BF16)


def conv(pad_ref, prior, rows, taps):
    count = rows.shape[0]
    pad_ref[0:8, :] = prior
    pad_ref[8 : 8 + count, :] = rows
    taps = taps.astype(F32) * 0.5
    running = taps[0:1] * pad_ref[5 : 5 + count, :]
    for j in range(1, 4):
        running = running + taps[j : j + 1] * pad_ref[5 + j : 5 + j + count, :]
    return silu_of_twice(running).astype(BF16)


def edge_sums(prior, rows, taps):
    both = jnp.concatenate([prior, rows], axis=0)
    taps = taps.astype(F32) * 0.5
    running = taps[0:1] * both[5:13]
    for j in range(1, 4):
        running = running + taps[j : j + 1] * both[5 + j : 13 + j]
    return running


def steps_of(step, bias, fading):
    step = step.astype(F32).T
    size = softplus(step + bias)
    decay = -size * jnp.exp(fading)
    count = step.shape[0]
    row = lax.broadcasted_iota(jnp.int32, (count, count), 0)
    col = lax.broadcasted_iota(jnp.int32, (count, count), 1)
    lower = (row >= col).astype(BF16)
    pieces = jnp.concatenate(split3(decay), axis=1)
    sums = jnp.dot(lower, pieces, preferred_element_type=F32)
    heads = step.shape[1]
    cumulative = sums[:, :heads] + sums[:, heads : 2 * heads] + sums[:, 2 * heads :]
    return size, cumulative


def lanes(block, width=WIDE):
    return pl.ds(pl.multiple_of(block * width, width), width)


def weights_of(step, bias, fading):
    size, cumulative = steps_of(step, bias, fading)
    last = cumulative[-1:]
    high, middle, _ = split3(size * jnp.exp(last - cumulative))
    return jnp.concatenate([high, middle], axis=1), last


def whole(value):
    return pl.BlockSpec(value.shape, lambda *_: (0,) * value.ndim)


def own_kernel(
    core_ref, x_ref, b_ref, ct_ref, step_ref, kx_ref, kb_ref, bias_ref, fading_ref,
    u_ref, first_weight_ref, closing_ref, tail_ref, pad, weight,
):
    n = pl.program_id(0)
    core = core_ref[0]
    heads = step_ref.shape[0]
    per_group = u_ref.shape[0] // 2
    end = slice(BLOCK - 16, BLOCK)
    x_width, b_width = x_ref.shape[1], b_ref.shape[1]
    tail_ref[:, lanes(n, x_width)] = x_ref[end, :]
    tail_ref[:, lanes(2 * x_width // b_width + n, b_width)] = b_ref[end, :]
    tail_ref[:, 2 * (x_width + b_width) :] = ct_ref[...]

    @pl.when(n == 0)
    def _():
        value, last = weights_of(step_ref[...], bias_ref[...], fading_ref[...])
        first_weight_ref[...] = value[0:16]
        closing_ref[...] = jnp.broadcast_to(last, (8, heads))
        row = lax.broadcasted_iota(jnp.int32, value.shape, 0)
        weight[...] = jnp.where(row < 8, 0.0, value.astype(F32)).astype(BF16)

    none = jnp.zeros((8, STATE), F32)
    b_t = conv(pad.at[0], none, b_ref[...].astype(F32), kb_ref[...]).astype(F32).T.astype(BF16)
    for j in range(per_group):
        block = 2 * j + core
        at = lanes(block)
        x_conv = conv(pad.at[j % 2], none, x_ref[:, at].astype(F32), kx_ref[:, at]).astype(F32)
        select = spread(2 * heads, WIDE, (2 * per_group * n + block) * HB, heads)
        inputs = x_conv * jnp.dot(weight[...], select, preferred_element_type=F32)
        u_ref[n * per_group + j] = jnp.dot(b_t, inputs.astype(BF16), preferred_element_type=F32)


def own_updates(core, x, b, c, step, kernel_x, kernel_b, bias, fading):
    heads = step.shape[0]
    groups = b.shape[1] // STATE
    width = x.shape[1] // groups
    blocks = x.shape[1] // WIDE // 2
    one = lambda n, c: (0, n)
    return pl.pallas_call(
        own_kernel,
        grid_spec=pltpu.PrefetchScalarGridSpec(
            num_scalar_prefetch=1,
            grid=(groups,),
            in_specs=[
                pl.BlockSpec((BLOCK, width), one),
                pl.BlockSpec((BLOCK, STATE), one),
                pl.BlockSpec((16, c.shape[1]), lambda n, s: (BLOCK // 16 - 1, 0)),
                whole(step),
                pl.BlockSpec((4, width), one),
                pl.BlockSpec((4, STATE), one),
                whole(bias),
                whole(fading),
            ],
            out_specs=[IN_VMEM, IN_VMEM, IN_VMEM, IN_VMEM],
            scratch_shapes=[
                pltpu.VMEM((2, BLOCK + 8, WIDE), F32),
                pltpu.VMEM((BLOCK, 2 * heads), BF16),
            ],
        ),
        out_shape=[
            pltpu.VMEM((blocks, STATE, WIDE), F32),
            pltpu.VMEM((16, 2 * heads), BF16),
            pltpu.VMEM((8, heads), F32),
            pltpu.VMEM((16, x.shape[1] + b.shape[1] + c.shape[1]), BF16),
        ],
        compiler_params=pltpu.CompilerParams(vmem_limit_bytes=VMEM),
        cost_estimate=pl.CostEstimate(flops=300_000_000, bytes_accessed=10_000_000, transcendentals=600_000),
        name="own_updates",
    )(core, hbm(x), hbm(b), hbm(c), hbm(step), hbm(kernel_x), hbm(kernel_b), hbm(bias), hbm(fading))


def chip_kernel(
    core_ref, u_own_ref, first_weight_ref, closing_ref, xh_ref, xt_ref, bh_ref, bt_ref, xr_ref, br_ref,
    sr_ref, kx_ref, kb_ref, bias_ref, fading_ref,
    u_ref, first_ref, decay_ref, edge_ref, pad, small, extra, weight, weight_first, values,
):
    n = pl.program_id(0)
    core = core_ref[0]
    even = core == 0
    heads = sr_ref.shape[0]
    per_group = u_ref.shape[0]
    head8 = slice(0, 8)
    tail8 = slice(8, 16)

    @pl.when(n == 0)
    def _():
        value, last = weights_of(sr_ref[...], bias_ref[...], fading_ref[...])
        row = lax.broadcasted_iota(jnp.int32, value.shape, 0)
        weight[...] = jnp.where((row < 3) & jnp.logical_not(even), 0.0, value.astype(F32)).astype(BF16)
        mine = first_weight_ref[...].astype(F32)
        row = lax.broadcasted_iota(jnp.int32, mine.shape, 0)
        dropped = (row >= 8) | ((row < 3) & even)
        weight_first[...] = jnp.where(dropped, 0.0, mine).astype(BF16)
        edge = jnp.where(even, mine, value[0:16].astype(F32))
        edge = edge[:, :heads] + edge[:, heads:]
        own = jnp.exp(closing_ref[0:1, :])
        other = jnp.exp(last)
        values[0:1, :] = own
        values[1:2, :] = other
        values[2:3, :] = jnp.exp(closing_ref[0:1, :] + last)
        values[3:6, :] = edge[0:3] * jnp.where(even, other, own)
        values[6:9, :] = edge[0:3]
        values[9:16, :] = jnp.zeros((7, heads), F32)

    def edges(own_head, own_end, recv_head, recv_end, taps):
        none = jnp.zeros(own_head.shape, F32)
        first = edge_sums(none, jnp.where(even, own_head, recv_head), taps)
        last = edge_sums(jnp.where(even, recv_end, own_end), none, taps)
        return jnp.where(even, none, recv_end), jnp.where(even, own_end, none), first, last

    def rows_of(ref, rows, at):
        return ref[rows, at].astype(F32)

    end = slice(BLOCK - 16, BLOCK)
    at = lanes(n, STATE)
    everything = slice(None)
    prior_own, prior_recv, b_first, b_last = edges(
        rows_of(bh_ref, slice(0, 16), everything)[head8],
        rows_of(bt_ref, slice(0, 16), everything)[tail8],
        rows_of(br_ref, slice(0, 16), at)[head8],
        rows_of(br_ref, end, at)[tail8],
        kb_ref[...],
    )
    b_own = conv(small.at[0], prior_own, bh_ref[...].astype(F32), kb_ref[...])
    b_recv = conv(pad.at[0], prior_recv, br_ref[:, at].astype(F32), kb_ref[...])
    b_own = b_own.astype(F32).T.astype(BF16)
    b_recv = b_recv.astype(F32).T.astype(BF16)
    pieces = jnp.concatenate(split3(values[...]), axis=1)
    for j in range(per_group):
        block = 2 * j + core
        head = (2 * per_group * n + block) * HB
        here = lanes(block)
        at = lanes(2 * per_group * n + block)
        taps = kx_ref[:, here]
        select = spread(2 * heads, WIDE, head, heads)
        prior_own, prior_recv, x_first, x_last = edges(
            rows_of(xh_ref, slice(0, 16), here)[head8],
            rows_of(xt_ref, slice(0, 16), here)[tail8],
            rows_of(xr_ref, slice(0, 16), at)[head8],
            rows_of(xr_ref, end, at)[tail8],
            taps,
        )
        x_own = conv(small.at[j % 2], prior_own, xh_ref[:, here].astype(F32), taps).astype(F32)
        x_own = x_own * jnp.dot(weight_first[...], select, preferred_element_type=F32)
        x_conv = conv(pad.at[j % 2], prior_recv, xr_ref[:, at].astype(F32), taps).astype(F32)
        inputs = x_conv * jnp.dot(weight[...], select, preferred_element_type=F32)
        u_recv = jnp.dot(b_recv, inputs.astype(BF16), preferred_element_type=F32)
        u_own = u_own_ref[n * per_group + j] + jnp.dot(
            b_own, x_own.astype(BF16), preferred_element_type=F32
        )
        wide = jnp.dot(pieces, spread(3 * heads, WIDE, head, heads), preferred_element_type=F32)
        own_factor = jnp.where(even, wide[1:2], 1.0)
        recv_factor = jnp.where(even, 1.0, wide[0:1])
        u_ref[j, 0:STATE, :] = (u_own * own_factor + u_recv * recv_factor).astype(BF16)
        first_ref[j] = jnp.where(even, u_own, u_recv).astype(BF16)
        decay_ref[j] = jnp.broadcast_to(jnp.where(even, wide[0:1], wide[1:2]), (8, WIDE))
        high, middle, low = split3(wide[2:3])
        place = lax.broadcasted_iota(jnp.int32, (1, WIDE), 1) % HEAD_DIM // 8
        packed = jnp.zeros((1, WIDE), F32)
        for q, value in enumerate((high, middle, low, wide[3:4], wide[4:5], wide[5:6])):
            packed = jnp.where(place == q, value.astype(F32), packed)
        extra[0:1, :] = packed
        extra[1:4, :] = x_first[0:3]
        extra[4:7, :] = x_last[0:3]
        extra[7:10, :] = b_first[0:3]
        extra[10:13, :] = b_last[0:3]
        extra[13:16, :] = jnp.zeros((3, WIDE), F32)
        u_ref[j, STATE : STATE + 16, :] = extra[...].astype(BF16)
        edge_ref[j, 0:3, :] = x_first[0:3]
        edge_ref[j, 3:6, :] = b_first[0:3]
        edge_ref[j, 6:9, :] = wide[6:9]
        edge_ref[j, 9:16, :] = jnp.zeros((7, WIDE), F32)


def chip_updates(core, own, x, b, x_recv, b_recv, step_recv, kernel_x, kernel_b, bias, fading):
    u_own, first_weight, closing = own
    heads = step_recv.shape[0]
    groups = b.shape[1] // STATE
    width = x.shape[1] // groups
    blocks = x.shape[1] // WIDE // 2
    per_group = blocks // groups
    end = BLOCK // 16 - 1
    one = lambda n, c: (0, n)
    tail = lambda n, c: (end, n)
    out = lambda n, c: (n, 0, 0)
    return pl.pallas_call(
        chip_kernel,
        grid_spec=pltpu.PrefetchScalarGridSpec(
            num_scalar_prefetch=1,
            grid=(groups,),
            in_specs=[
                IN_VMEM,
                IN_VMEM,
                IN_VMEM,
                pl.BlockSpec((16, width), one),
                pl.BlockSpec((16, width), tail),
                pl.BlockSpec((16, STATE), one),
                pl.BlockSpec((16, STATE), tail),
                IN_VMEM,
                IN_VMEM,
                IN_VMEM,
                pl.BlockSpec((4, width), one),
                pl.BlockSpec((4, STATE), one),
                whole(bias),
                whole(fading),
            ],
            out_specs=[
                pl.BlockSpec((per_group, STATE + 16, WIDE), out),
                pl.BlockSpec((per_group, STATE, WIDE), out),
                pl.BlockSpec((per_group, 8, WIDE), out),
                pl.BlockSpec((per_group, 16, WIDE), out),
            ],
            scratch_shapes=[
                pltpu.VMEM((2, BLOCK + 8, WIDE), F32),
                pltpu.VMEM((2, 24, WIDE), F32),
                pltpu.VMEM((16, WIDE), F32),
                pltpu.VMEM((BLOCK, 2 * heads), BF16),
                pltpu.VMEM((16, 2 * heads), BF16),
                pltpu.VMEM((16, heads), F32),
            ],
        ),
        out_shape=[
            pltpu.HBM((blocks, STATE + 16, WIDE), BF16),
            pltpu.HBM((blocks, STATE, WIDE), BF16),
            pltpu.HBM((blocks, 8, WIDE), F32),
            pltpu.HBM((blocks, 16, WIDE), F32),
        ],
        compiler_params=pltpu.CompilerParams(vmem_limit_bytes=VMEM),
        cost_estimate=pl.CostEstimate(flops=300_000_000, bytes_accessed=10_000_000, transcendentals=600_000),
        name="chip_updates",
    )(
        core, vmem(u_own), vmem(first_weight), vmem(closing), hbm(x), hbm(x), hbm(b), hbm(b), vmem(x_recv),
        vmem(b_recv), vmem(step_recv), hbm(kernel_x), hbm(kernel_b), hbm(bias), hbm(fading),
    )


def edge_kernel(core_ref, first_ref, edge_ref, he_ref, ho_ref, kx_ref, kb_ref, out_ref):
    n = pl.program_id(0)
    core = core_ref[0]
    even = core == 0
    per_group = first_ref.shape[0]
    blocks = 2 * per_group * pl.num_programs(0)
    none = jnp.zeros((8, WIDE), F32)
    row = lax.broadcasted_iota(jnp.int32, (16, WIDE), 0)

    def from_halo(at, taps):
        halo = jnp.where(even, he_ref[:, at].astype(F32), ho_ref[:, at].astype(F32))[8:]
        return edge_sums(halo, none, taps)[0:3]

    b_sums = from_halo(lanes(blocks + n, STATE), kb_ref[...])
    for j in range(per_group):
        block = 2 * j + core
        x_sums = from_halo(lanes(2 * per_group * n + block), kx_ref[:, lanes(block)])
        rows = edge_ref[j]
        x_conv = silu_of_twice(rows[0:3] + x_sums).astype(BF16).astype(F32)
        b_conv = silu_of_twice(rows[3:6] + b_sums)
        inputs = x_conv * rows[6:9]
        pad = jnp.zeros((13, WIDE), F32)
        inputs = jnp.concatenate([inputs, pad], axis=0).astype(BF16)
        b_conv = jnp.concatenate([b_conv, pad], axis=0).astype(BF16)
        term = lax.dot_general(b_conv, inputs, (((0,), (0,)), ((), ())), preferred_element_type=F32)
        out_ref[j] = (first_ref[j].astype(F32) + term).astype(BF16)


def whole_first(core, first, edge, halo_even, halo_odd, kernel_x, kernel_b):
    groups = kernel_b.shape[1] // STATE
    per_group = first.shape[0] // groups
    width = kernel_x.shape[1] // groups
    out = lambda n, c: (n, 0, 0)
    one = lambda n, c: (0, n)
    return pl.pallas_call(
        edge_kernel,
        grid_spec=pltpu.PrefetchScalarGridSpec(
            num_scalar_prefetch=1,
            grid=(groups,),
            in_specs=[
                pl.BlockSpec((per_group, STATE, WIDE), out),
                pl.BlockSpec((per_group, 16, WIDE), out),
                whole(halo_even),
                whole(halo_odd),
                pl.BlockSpec((4, width), one),
                pl.BlockSpec((4, STATE), one),
            ],
            out_specs=pl.BlockSpec((per_group, STATE, WIDE), out),
        ),
        out_shape=pltpu.HBM(first.shape, BF16),
        compiler_params=pltpu.CompilerParams(vmem_limit_bytes=SMALL),
        cost_estimate=pl.CostEstimate(flops=30_000_000, bytes_accessed=3_000_000, transcendentals=10_000),
        name="whole_first",
    )(core, hbm(first), hbm(edge), hbm(halo_even), hbm(halo_odd), hbm(kernel_x), hbm(kernel_b))


def within_kernel(
    core_ref, x_ref, gate_ref, b_ref, c_ref, step_ref, halo_ref, tx_ref, tb_ref, tc_ref,
    kx_ref, kb_ref, kc_ref, bias_ref, fading_ref, a_ref, g_ref, cc_ref, pad, pieces, cum_t, scores, cross, x_step,
):
    k = pl.program_id(0)
    even = core_ref[0] == 0
    heads = step_ref.shape[0]
    half = BLOCK // 2
    steps = pl.num_programs(0)
    blocks = x_ref.shape[1] // WIDE
    group = k // (steps // 2)

    def prior(halo_at, tail_ref, at):
        halo = halo_ref[:, lanes(halo_at)].astype(F32)
        return jnp.where(even, halo, tail_ref[:, lanes(at)].astype(F32))[8:]

    @pl.when(k == 0)
    def _():
        size, cumulative = steps_of(step_ref[...], bias_ref[...], fading_ref[...])
        cumulative = cumulative * LOG2E
        pieces[0] = jnp.concatenate(split3(cumulative), axis=1)
        pieces[1] = jnp.concatenate(split3(size), axis=1)
        turned = cumulative.T
        for n in range(heads // HB):
            cum_t[n, 0:HB, :] = turned[n * HB : (n + 1) * HB]

    @pl.when(k % (steps // 2) == 0)
    def _():
        in_halo = steps * blocks + group
        b_conv = conv(pad.at[0], prior(in_halo, tb_ref, group), b_ref[...].astype(F32), kb_ref[...])
        c_conv = conv(pad.at[1], prior(in_halo + 2, tc_ref, group), c_ref[...].astype(F32), kc_ref[...])
        cc_ref[...] = c_conv
        products = lax.dot_general(
            c_conv, b_conv, (((1,), (1,)), ((), ())), preferred_element_type=F32
        )
        row = lax.broadcasted_iota(jnp.int32, (half, half), 0)
        col = lax.broadcasted_iota(jnp.int32, (half, half), 1)
        for a in range(2):
            at = slice(a * half, (a + 1) * half)
            scores[at, :] = jnp.where(row >= col, products[at, at], 0.0)
        cross[...] = products[half:, :half].astype(BF16)

    for m in range(blocks):
        block = k * blocks + m
        here = slice(m * WIDE, (m + 1) * WIDE)
        select = spread(3 * heads, WIDE, block * HB, heads)
        cum_wide = jnp.dot(pieces[0], select, preferred_element_type=F32)
        step_wide = jnp.dot(pieces[1], select, preferred_element_type=F32)
        rows = x_ref[:, here].astype(F32)
        x_conv = conv(pad.at[m % 2], prior(block, tx_ref, block), rows, kx_ref[:, here]).astype(F32)
        stepped = x_conv * step_wide
        x_step[m % 2] = stepped.astype(BF16)
        lines = cum_t[block]
        middle = cum_wide[half - 1 : half]
        scaled = (stepped[:half] * jnp.exp2(middle - cum_wide[:half])).astype(BF16)
        late = jnp.dot(cross[...], scaled, preferred_element_type=F32)
        late = late * jnp.exp2(cum_wide[half:] - middle)
        gate = silu_of_twice(gate_ref[:, here].astype(F32) * 0.5)
        g_ref[:, here] = (jnp.exp2(cum_wide) * gate).astype(BF16)
        for a in range(2):
            at = slice(a * half, (a + 1) * half)
            parts = []
            for j in range(HB):
                column = cum_wide[at, j * HEAD_DIM : j * HEAD_DIM + 1]
                line = lines[j : j + 1, at]
                weights = scores[at, :] * jnp.exp2(jnp.minimum(column - line, 0.0))
                parts.append(
                    jnp.dot(
                        weights.astype(BF16),
                        x_step[m % 2, at, j * HEAD_DIM : (j + 1) * HEAD_DIM],
                        preferred_element_type=F32,
                    )
                )
            inside = jnp.concatenate(parts, axis=1)
            if a == 1:
                inside = inside + late
            a_ref[at, here] = (inside * gate[at]).astype(BF16)


def within_block(core, x, gate, b, c, step, halo, x_recv, b_recv, c_recv, kernel_x, kernel_b, kernel_c, bias, fading):
    heads = step.shape[0]
    width = 4 * WIDE
    steps = x.shape[1] // width
    per_group = steps // (b.shape[1] // STATE)
    full = lambda k, s: (0, 0)
    end = BLOCK // 16 - 1
    group = lambda k, s: (0, k // per_group)
    one = lambda k, s: (0, k)
    return pl.pallas_call(
        within_kernel,
        grid_spec=pltpu.PrefetchScalarGridSpec(
            num_scalar_prefetch=1,
            grid=(steps,),
            in_specs=[
                pl.BlockSpec((BLOCK, width), one),
                pl.BlockSpec((BLOCK, width), one),
                pl.BlockSpec((BLOCK, STATE), group),
                pl.BlockSpec((BLOCK, STATE), group),
                whole(step),
                whole(halo),
                *[pl.BlockSpec((16, v.shape[1]), lambda k, s: (end, 0)) for v in (x_recv, b_recv, c_recv)],
                pl.BlockSpec((4, width), one),
                pl.BlockSpec((4, STATE), group),
                pl.BlockSpec((4, STATE), group),
                pl.BlockSpec((1, heads), full),
                pl.BlockSpec((1, heads), full),
            ],
            out_specs=[
                pl.BlockSpec((BLOCK, width), one),
                pl.BlockSpec((BLOCK, width), one),
                pl.BlockSpec((BLOCK, STATE), group),
            ],
            scratch_shapes=[
                pltpu.VMEM((2, BLOCK + 8, WIDE), F32),
                pltpu.VMEM((2, BLOCK, 3 * heads), BF16),
                pltpu.VMEM((heads // HB, 8, BLOCK), F32),
                pltpu.VMEM((BLOCK, BLOCK // 2), F32),
                pltpu.VMEM((BLOCK // 2, BLOCK // 2), BF16),
                pltpu.VMEM((2, BLOCK, WIDE), BF16),
            ],
        ),
        out_shape=[
            jax.ShapeDtypeStruct(x.shape, BF16),
            jax.ShapeDtypeStruct(x.shape, BF16),
            jax.ShapeDtypeStruct(c.shape, BF16),
        ],
        compiler_params=pltpu.CompilerParams(vmem_limit_bytes=VMEM),
        cost_estimate=pl.CostEstimate(flops=8_000_000_000, bytes_accessed=12_000_000, transcendentals=6_000_000),
        name="within_block",
    )(
        core, hbm(x), hbm(gate), hbm(b), hbm(c), hbm(step), hbm(halo), hbm(x_recv), hbm(b_recv),
        hbm(c_recv), hbm(kernel_x), hbm(kernel_b), hbm(kernel_c), hbm(bias), hbm(fading),
    )


def scan_kernel(gathered_ref, _, starts_ref, final_ref, decays, inputs, b_rows):
    chips, part, _ = starts_ref.shape
    r = pl.program_id(0)

    @pl.when(r == 0)
    def _():
        extra = [gathered_ref[n, STATE : STATE + 16, :].astype(F32) for n in range(chips)]
        packed = jnp.concatenate([value[0:1] for value in extra], axis=0).astype(BF16)
        row = lax.broadcasted_iota(jnp.int32, (WIDE, WIDE), 0)
        col = lax.broadcasted_iota(jnp.int32, (WIDE, WIDE), 1)
        wide = [
            jnp.dot(packed, (row == col // HEAD_DIM * HEAD_DIM + 8 * q).astype(BF16), preferred_element_type=F32)
            for q in range(6)
        ]
        decays[...] = wide[0] + wide[1] + wide[2]
        pad = jnp.zeros((13, WIDE), F32)
        for n in range(chips):
            x_sums, b_sums = extra[n][1:4], extra[n][7:10]
            if n:
                x_sums = x_sums + extra[n - 1][4:7]
                b_sums = b_sums + extra[n - 1][10:13]
            x_conv = silu_of_twice(x_sums).astype(BF16).astype(F32)
            weight = jnp.concatenate([wide[3 + t][n : n + 1] for t in range(3)], axis=0)
            inputs[n] = jnp.concatenate([x_conv * weight, pad], axis=0).astype(BF16)
            b_rows[n] = jnp.concatenate([silu_of_twice(b_sums), pad], axis=0).astype(BF16)

    rows = pl.ds(pl.multiple_of(r * part, part), part)
    state = jnp.zeros((part, WIDE), F32)
    for n in range(chips):
        starts_ref[n] = state.astype(BF16)
        term = lax.dot_general(
            b_rows[n, :, rows], inputs[n], (((0,), (0,)), ((), ())), preferred_element_type=F32
        )
        state = state * decays[n : n + 1, :] + (gathered_ref[n, rows, :].astype(F32) + term)
    final_ref[rows, :] = state


def scan_states(gathered, after):
    chips = gathered.shape[0]
    part = STATE // 2
    return pl.pallas_call(
        scan_kernel,
        grid=(2,),
        in_specs=[IN_VMEM, IN_HBM],
        out_specs=[pl.BlockSpec((chips, part, WIDE), lambda r: (0, r, 0)), IN_VMEM],
        out_shape=[
            pltpu.HBM((chips, STATE, WIDE), BF16),
            pltpu.VMEM((STATE, WIDE), F32),
        ],
        scratch_shapes=[
            pltpu.VMEM((chips, WIDE), F32),
            pltpu.VMEM((chips, 16, WIDE), BF16),
            pltpu.VMEM((chips, 16, STATE), BF16),
        ],
        compiler_params=pltpu.CompilerParams(vmem_limit_bytes=SMALL),
        cost_estimate=pl.CostEstimate(flops=20_000_000, bytes_accessed=2_500_000, transcendentals=0),
        name="scan_states",
    )(vmem(gathered), hbm(after))


def start_kernel(core_ref, start_ref, first_ref, decay_ref, _, keep_ref, send_ref):
    even = core_ref[0] == 0
    for j in range(first_ref.shape[0]):
        n = pl.program_id(0) * first_ref.shape[0] + j
        start = start_ref[n].astype(F32)
        later = start * decay_ref[j, 0:1, :] + first_ref[j].astype(F32)
        keep_ref[n] = jnp.where(even, start, later).astype(BF16)
        send_ref[n] = jnp.where(even, later, start).astype(BF16)


def block_starts(core, chip_start, first_update, first_decay, after):
    shape = pltpu.VMEM(chip_start.shape, BF16)
    return pl.pallas_call(
        start_kernel,
        grid=(chip_start.shape[0] // 4,),
        in_specs=[
            pl.BlockSpec(memory_space=pltpu.SMEM),
            IN_VMEM,
            pl.BlockSpec((4, STATE, WIDE), lambda i: (i, 0, 0)),
            pl.BlockSpec((4, 8, WIDE), lambda i: (i, 0, 0)),
            IN_HBM,
        ],
        out_specs=[IN_VMEM, IN_VMEM],
        out_shape=[shape, shape],
        compiler_params=pltpu.CompilerParams(vmem_limit_bytes=SMALL),
        cost_estimate=pl.CostEstimate(flops=2_000_000, bytes_accessed=4_500_000, transcendentals=0),
        name="block_starts",
    )(core, vmem(chip_start), hbm(first_update), hbm(first_decay), hbm(after))


def carried_rows(n, block, rows, c_conv, state, a_ref, g_ref, width):
    at = pl.ds(pl.multiple_of(n * width + block * WIDE, WIDE), WIDE)
    carried = jnp.dot(c_conv, state, preferred_element_type=F32)
    return a_ref[rows, at].astype(F32) + carried * g_ref[rows, at].astype(F32)


def near_kernel(core_ref, a_ref, g_ref, cc_ref, keep_ref, y_ref, sum_ref):
    n = pl.program_id(0)
    groups = pl.num_programs(0)
    per_group = keep_ref.shape[0] // groups
    width = a_ref.shape[1] // groups
    everything = slice(None)
    c_conv = cc_ref[:, lanes(n, STATE)]
    total = jnp.zeros((BLOCK, 1), F32)
    for j in range(per_group):
        at = n * per_group + j
        block = 2 * j + core_ref[0]
        y = carried_rows(n, block, everything, c_conv, keep_ref[at], a_ref, g_ref, width)
        y_ref[:, lanes(at)] = y
        total = total + jnp.sum(y * y, axis=1, keepdims=True)
    sum_ref[n] = jnp.broadcast_to(total, sum_ref.shape[1:])


def near_rows(core, a, g, cc, keep):
    tokens, channels = a.shape
    groups = cc.shape[1] // STATE
    smem = pl.BlockSpec(memory_space=pltpu.SMEM)
    return pl.pallas_call(
        near_kernel,
        grid=(groups,),
        in_specs=[smem, IN_VMEM, IN_VMEM, IN_VMEM, IN_VMEM],
        out_specs=[IN_VMEM, IN_VMEM],
        out_shape=[pltpu.VMEM((tokens, channels // 2), F32), pltpu.VMEM((groups, tokens, 128), F32)],
        compiler_params=pltpu.CompilerParams(vmem_limit_bytes=SMALL),
        cost_estimate=pl.CostEstimate(flops=300_000_000, bytes_accessed=5_000_000, transcendentals=1000),
        name="near_rows",
    )(core, vmem(a), vmem(g), vmem(cc), vmem(keep))


def finish_kernel(core_ref, a_ref, g_ref, cc_ref, near_ref, sum_ref, recv_ref, gain_ref, out_ref, y_ref):
    core = core_ref[0]
    rows, width = out_ref.shape
    n, r = pl.program_id(0), pl.program_id(1)
    at_rows = pl.ds(pl.multiple_of(r * rows, rows), rows)
    per_group = recv_ref.shape[0] // pl.num_programs(0)
    total = sum_ref[n, at_rows, 0:1]
    c_conv = cc_ref[at_rows, lanes(n, STATE)]
    for j in range(per_group):
        block = 2 * j + 1 - core
        y = carried_rows(n, block, at_rows, c_conv, recv_ref[n * per_group + j], a_ref, g_ref, width)
        y_ref[:, j * WIDE : (j + 1) * WIDE] = y
        total = total + jnp.sum(y * y, axis=1, keepdims=True)
    inverse = 1.0 / jnp.sqrt(total / width + epsilon)
    for j in range(per_group):
        near = near_ref[at_rows, lanes(n * per_group + j)]
        for y, block in ((near, 2 * j + core), (y_ref[:, j * WIDE : (j + 1) * WIDE], 2 * j + 1 - core)):
            out_ref[:, lanes(block)] = (y * inverse * gain_ref[:, lanes(block)]).astype(BF16)


def finish(core, a, g, cc, near, sums, recv, gain):
    tokens, channels = a.shape
    groups = cc.shape[1] // STATE
    width = channels // groups
    rows = tokens
    smem = pl.BlockSpec(memory_space=pltpu.SMEM)
    return pl.pallas_call(
        finish_kernel,
        grid=(groups, 1),
        in_specs=[smem] + [IN_VMEM] * 6 + [pl.BlockSpec((1, width), lambda n, r: (0, n))],
        out_specs=pl.BlockSpec((rows, width), lambda n, r: (r, n)),
        scratch_shapes=[pltpu.VMEM((rows, width // 2), F32)],
        out_shape=jax.ShapeDtypeStruct((tokens, channels), BF16),
        compiler_params=pltpu.CompilerParams(vmem_limit_bytes=SMALL),
        cost_estimate=pl.CostEstimate(flops=300_000_000, bytes_accessed=9_000_000, transcendentals=1000),
        name="finish",
    )(core, vmem(a), vmem(g), vmem(cc), vmem(near), vmem(sums), vmem(recv), gain)


def slots_kernel(owners_ref, rank_ref, state_ref, o0, o1, o2, o3):
    outs = (o0, o1, o2, o3)
    for out in outs:
        out[...] = jnp.zeros(out.shape, F32)
    for j in range(HB):
        owner = owners_ref[j]
        slot = jnp.int32(0)
        for i in range(j):
            slot = slot + (owners_ref[i] == owner).astype(jnp.int32)
        piece = state_ref[:, j * HEAD_DIM : (j + 1) * HEAD_DIM].T
        for d, out in enumerate(outs):
            for r in range(out.shape[0]):

                @pl.when((owner == rank_ref[0] ^ d) & (slot == r))
                def _(out=out, r=r, piece=piece):
                    out[r] = piece


def final_slots(owners, rank, state, dests, capacity):
    one = pltpu.VMEM((capacity, HEAD_DIM, STATE), F32)
    smem = pl.BlockSpec(memory_space=pltpu.SMEM)
    return pl.pallas_call(
        slots_kernel,
        in_specs=[smem, smem, IN_VMEM],
        out_specs=[IN_VMEM] * dests,
        out_shape=[one] * dests,
        compiler_params=pltpu.CompilerParams(vmem_limit_bytes=SMALL),
        name="final_slots",
    )(owners, rank, vmem(state))


def local(
    x_input, b_input, output_projection_input, step_input, gate_input, kernel_x, kernel_b, kernel_c,
    step_bias, fading_logarithm, norm_gain, owner_map,
):
    ctx_count = lax.axis_size("ctx")
    ctx_rank = lax.axis_index("ctx")
    dec_count = lax.axis_size("dec")
    dec_rank = lax.axis_index("dec")
    core = ctx_rank % 2
    core_arg = core.astype(jnp.int32).reshape(1)
    x = x_input[0]
    b = b_input[0]
    c = output_projection_input[0]
    step = step_input[0].T
    bias = step_bias.reshape(1, -1)
    fading = fading_logarithm.reshape(1, -1)

    swap = [(i, i ^ 1) for i in range(ctx_count)]
    x_recv, b_recv, step_recv = (
        lax.ppermute(x, "ctx", swap),
        lax.ppermute(b, "ctx", swap),
        lax.ppermute(step, "ctx", swap),
    )
    *own, tail = own_updates(core_arg, x, b, c, step, kernel_x, kernel_b, bias, fading)
    tail, step_recv = lax.optimization_barrier((tail, step_recv))
    from_even = lax.ppermute(tail, "ctx", [(i, i + 1) for i in range(1, ctx_count - 1, 2)])
    updates, first_update, first_decay, edge = chip_updates(
        core_arg, own, x, b, x_recv, b_recv, step_recv, kernel_x, kernel_b, bias, fading
    )
    c_recv = lax.ppermute(c, "ctx", swap)
    from_odd = lax.ppermute(from_even, "ctx", swap)
    updates, from_even = lax.optimization_barrier((updates, from_even))
    same_core = [[2 * i + j for i in range(ctx_count // 2)] for j in range(2)]
    gathered = lax.all_to_all(updates, "ctx", 0, 0, axis_index_groups=same_core, tiled=True)
    a, g, cc = within_block(
        core_arg, x, gate_input[0], b, c, step, from_even, x_recv, b_recv, c_recv,
        kernel_x, kernel_b, kernel_c, bias, fading,
    )
    first_update = whole_first(core_arg, first_update, edge, from_even, from_odd, kernel_x, kernel_b)
    starts, state = scan_states(gathered, cc)
    chip_start = lax.all_to_all(starts, "ctx", 0, 0, axis_index_groups=same_core, tiled=True)

    owners = lax.dynamic_slice_in_dim(owner_map[0, :, 0], ctx_rank * HB, HB)
    outgoing = final_slots(owners, dec_rank.astype(jnp.int32).reshape(1), state, dec_count, 2)
    arrived = jnp.zeros((dec_count,) + outgoing[0].shape, F32)
    for d in range(dec_count):
        piece = outgoing[d]
        if d:
            piece = lax.ppermute(piece, "dec", [(i, i ^ d) for i in range(dec_count)])
        arrived = lax.dynamic_update_index_in_dim(arrived, piece, dec_rank ^ d, 0)

    keep, send = block_starts(core_arg, chip_start, first_update, first_decay, arrived)
    recv = lax.ppermute(send, "ctx", swap)
    near, sums = near_rows(core_arg, a, g, cc, keep)
    recv, near, sums = lax.optimization_barrier((recv, near, sums))
    mixer_rows = finish(core_arg, a, g, cc, near, sums, recv, norm_gain.reshape(1, -1))
    return (mixer_rows[None], arrived[None, :, None])


def solution(mesh):
    return jax.shard_map(
        local,
        mesh=mesh,
        in_specs=(
            P("dec", "ctx", "tp"),
            P("dec", "ctx", "tp"),
            P("dec", "ctx", "tp"),
            P("dec", "ctx", "tp"),
            P("dec", "ctx", "tp"),
            P(None, "tp"),
            P(None, "tp"),
            P(None, "tp"),
            P("tp"),
            P("tp"),
            P("tp"),
            P("dec", "tp", None),
        ),
        out_specs=(P("dec", "ctx", "tp"), P("dec", None, ("tp", "ctx"), None, None, None)),
        check_vma=False,
    )
```
